256 devices in a mesh: seq: 32 (over x, z), tensor: 8 (over y, core).
Axes of the slice: x: 4, y: 4, z: 8, core: 2. Of those that a mesh axis runs over, the one named last changes fastest.
Arguments:
- queries: bfloat16 [4608, 3072], P('seq', 'tensor'), may hold values from -60 to 60
- keys: bfloat16 [4608, 3072], P('seq', 'tensor'), may hold values from -60 to 60
- values: bfloat16 [4608, 3072], P('seq', 'tensor'), may hold values from -60 to 60
- out_grad: bfloat16 [4608, 3072], P('seq', 'tensor'), may hold values from -60 to 60
Outputs:
- out_scaled: bfloat16 [4608, 3072], P('seq', 'tensor')
- dq_scaled: bfloat16 [4608, 3072], P('seq', 'tensor')
- dk_scaled: bfloat16 [4608, 3072], P('seq', 'tensor')
- dv_scaled: bfloat16 [4608, 3072], P('seq', 'tensor')
The draws below stay inside these ranges and needn't reach their ends.
All inputs are finite; a program needn't handle non-finite values. Where the reference program divides by a largest or mean magnitude, that divisor is 1e-20 or more.
Results may differ from the reference program's by a relative error of at most 0.019.
The reference program's roundings to bfloat16 on the way (of `weights` and `grad_scores`) count: a program that leaves them out, or rounds other values in their place, can miss the bound.
Values may be sent and summed in bfloat16 or wider, within the bound.
No kernel may reach another device: no remote copies, remote signals or barrier semaphores. Data moves between devices by JAX's collectives and lax.ppermute only.
A program may use at most 64 MiB of HBM per device.

```python
import math
import jax
import jax.numpy as jnp
from jax import lax

HEADS = 24
HD = 128
SEQLEN = 4608


def shaped(base, key, rise, level, col_low, col_high):
    row_key, col_key = jax.random.split(key)
    position = jnp.arange(SEQLEN, dtype=jnp.float32) / (SEQLEN - 1)
    row_scale = level * jnp.exp(position * math.log(rise)) * jax.random.uniform(row_key, (SEQLEN,), jnp.float32, 0.8, 1.25)
    col_scale = jnp.exp(jax.random.uniform(col_key, (HEADS * HD,), jnp.float32, math.log(col_low), math.log(col_high)))
    return base * row_scale[:, None] * col_scale[None, :]


def mixed_base(key):
    normal_key = jax.random.fold_in(key, 0)
    shape_pair = (SEQLEN, HEADS * HD)
    normal_part = jax.random.normal(normal_key, shape_pair, jnp.float32)
    return normal_part


def key_field(key, twin):
    key = jax.random.fold_in(key, 11)
    base_key, scale_key = jax.random.split(key)
    field = shaped(mixed_base(base_key), scale_key, 1.0 / 3.0, 1.8, 0.5, 2.0)
    earlier = jnp.roll(field, 1, axis=0)
    row_index = jnp.arange(SEQLEN)
    mixing = jnp.where(row_index % 41 == 1, twin, 0.0)[:, None]
    return mixing * earlier + jnp.sqrt(1.0 - mixing * mixing) * field


def draw_keys(key, part):
    field = key_field(key, 0.0)
    return jnp.clip(field, -60.0, 60.0).astype(jnp.bfloat16)


def draw_queries(key, part):
    own_key = jax.random.fold_in(key, 5)
    base_key, scale_key = jax.random.split(own_key, 2)
    field = shaped(mixed_base(base_key), scale_key, 3.0, 0.6, 0.5, 2.0)
    return jnp.clip(field, -60.0, 60.0).astype(jnp.bfloat16)


def draw_values(key, part):
    key = jax.random.fold_in(key, 3)
    base_key, scale_key = jax.random.split(key)
    field = shaped(mixed_base(base_key), scale_key, 3.0, 1.0, 1.0, 10.0)
    return jnp.clip(field, -60.0, 60.0).astype(jnp.bfloat16)


def draw_out_grad(key, part):
    key = jax.random.fold_in(key, 7)
    base_key, scale_key = jax.random.split(key)
    field = shaped(mixed_base(base_key), scale_key, 3.0, 1.0, 1.0, 10.0)
    return jnp.clip(field, -60.0, 60.0).astype(jnp.bfloat16)


def setup_inputs(seed: int = 0) -> dict:
    seeds = jax.random.split(jax.random.key(seed), 5)
    queries = draw_queries(jax.random.fold_in(seeds[4], 71), 0)
    keys = draw_keys(jax.random.fold_in(seeds[4], 71), 0)
    values = draw_values(jax.random.fold_in(seeds[4], 71), 0)
    out_grad = draw_out_grad(jax.random.fold_in(seeds[4], 71), 0)
    return dict(queries=queries, keys=keys, values=values, out_grad=out_grad)


TOP = 4.0

def peak_of(tensor):
    return jnp.max(jnp.abs(tensor.astype(jnp.float32)))

def to_scaled(tensor, peak):
    return (tensor.astype(jnp.float32) * (TOP / peak)).astype(jnp.bfloat16)

def heads_first(tensor):
    return jnp.transpose(tensor.reshape(SEQLEN, HEADS, HD), (1, 0, 2))

def rows_first(cube):
    return jnp.transpose(cube, (1, 0, 2)).reshape(SEQLEN, HEADS * HD)

def reference(queries, keys, values, out_grad):
    peak_q = peak_of(queries)
    peak_k = peak_of(keys)
    peak_v = peak_of(values)
    peak_g = peak_of(out_grad)
    query_cube = heads_first(to_scaled(queries, peak_q))
    key_cube = heads_first(to_scaled(keys, peak_k))
    value_cube = heads_first(to_scaled(values, peak_v))
    grad_cube = heads_first(to_scaled(out_grad, peak_g))
    root_dim = math.sqrt(HD)
    score_scale = peak_q * peak_k / (TOP * TOP * root_dim)
    grad_scale = peak_g * peak_v / (TOP * TOP)

    def one_head(inputs):
        query_head, key_head, value_head, grad_head = inputs
        scores = jnp.dot(query_head, key_head.T, preferred_element_type=jnp.float32) * score_scale
        row_max = lax.optimization_barrier(jnp.max(scores, axis=1, keepdims=True))
        weights = jnp.exp(scores - row_max)
        row_total = lax.optimization_barrier(jnp.sum(weights, axis=1, keepdims=True))
        attended = jnp.dot(weights.astype(jnp.bfloat16), value_head, preferred_element_type=jnp.float32) / row_total * (peak_v / TOP)
        log_total = row_max + jnp.log(row_total)
        grad_rows = grad_head.astype(jnp.float32) * (peak_g / TOP)
        row_delta = lax.optimization_barrier(jnp.sum(grad_rows * attended, axis=1, keepdims=True))
        probs = jnp.exp(scores - log_total)
        grad_probs = jnp.dot(grad_head, value_head.T, preferred_element_type=jnp.float32) * grad_scale
        grad_scores = (probs * (grad_probs - row_delta)).astype(jnp.bfloat16)
        grad_v = jnp.dot(probs.astype(jnp.bfloat16).T, grad_head, preferred_element_type=jnp.float32) * (peak_g / TOP)
        grad_q = jnp.dot(grad_scores, key_head, preferred_element_type=jnp.float32) * (peak_k / (TOP * root_dim))
        grad_k = jnp.dot(grad_scores.T, query_head, preferred_element_type=jnp.float32) * (peak_q / (TOP * root_dim))
        return (attended, grad_q, grad_k, grad_v)
    attended, grad_q, grad_k, grad_v = lax.map(one_head, (query_cube, key_cube, value_cube, grad_cube))
    results = []
    for cube in (attended, grad_q, grad_k, grad_v):
        flat = rows_first(cube)
        results.append((flat * (TOP / jnp.max(jnp.abs(flat)))).astype(jnp.bfloat16))
    return (results[0], results[1], results[2], results[3])
```

```python
import functools
import math

import jax
import jax.numpy as jnp
from jax import lax
from jax.experimental import pallas as pl
from jax.experimental.pallas import tpu as pltpu
from jax.sharding import Mesh
from jax.sharding import PartitionSpec as P

HD = 128
TOP = 4.0
ROOT = math.sqrt(HD)
NT = (((1,), (1,)), ((), ()))
TN = (((0,), (0,)), ((), ()))
NN = (((1,), (0,)), ((), ()))
F32 = jnp.float32
BF16 = jnp.bfloat16
VMEM_LIMIT = 48 * 1024 * 1024


def mxu(a, b, dims):
    return lax.dot_general(a, b, dims, preferred_element_type=F32)


def call(body, name, out_shape, args, scratch=(), flops=0, nbytes=0, exps=0):
    return pl.pallas_call(
        body,
        name=name,
        out_shape=out_shape,
        scratch_shapes=list(scratch),
        compiler_params=pltpu.CompilerParams(vmem_limit_bytes=VMEM_LIMIT),
        cost_estimate=pl.CostEstimate(flops=flops, bytes_accessed=nbytes, transcendentals=exps),
    )(*args)


def lanes_of(values):
    lane = lax.broadcasted_iota(jnp.int32, (1, 128), 1)
    row = jnp.zeros((1, 128), F32)
    for i, value in enumerate(values):
        row = jnp.where(lane == i, value, row)
    return row


def peak_lanes(ref):
    return jnp.max(ref[...], axis=0)


def biggest(x):
    return jnp.max(jnp.abs(x.astype(F32)), keepdims=True)


def prep_kernel(q_ref, k_ref, v_ref, g_ref, qg_ref, kv_ref, pk_ref):
    width = q_ref.shape[1]
    qg_ref[:, :width] = q_ref[...]
    qg_ref[:, width:] = g_ref[...]
    kv_ref[:, :width] = k_ref[...]
    kv_ref[:, width:] = v_ref[...]
    row = lanes_of([biggest(r[...]) for r in (q_ref, k_ref, v_ref, g_ref)])
    pk_ref[...] = jnp.broadcast_to(row[None], pk_ref.shape)


def scaled(x, factor):
    return (x.astype(F32) * factor).astype(BF16)


def load_keys(kv_refs, kb, vb, rk, rv):
    rows, width = kv_refs[0].shape[0], kb.shape[1]
    for s, ref in enumerate(kv_refs):
        kb[s * rows : (s + 1) * rows, :] = scaled(ref[:, :width], rk)
        vb[s * rows : (s + 1) * rows, :] = scaled(ref[:, width:], rv)


def forward_kernel(heads, tile, qg_ref, kv0, kv1, kv2, kv3, pk_ref, o_ref, st_ref, kb, vb):
    pk = peak_lanes(pk_ref)
    pq, pkk, pv, pg = (pk[:, i : i + 1] for i in range(4))
    load_keys((kv0, kv1, kv2, kv3), kb, vb, TOP / pkk, TOP / pv)
    score_scale = pq * pkk / (TOP * TOP * ROOT)
    width = heads * HD
    st_ref[...] = jnp.zeros_like(st_ref)
    for h in range(heads):
        cols = slice(h * HD, (h + 1) * HD)
        gcols = slice(width + h * HD, width + (h + 1) * HD)
        for t in range(qg_ref.shape[0] // tile):
            rows = slice(t * tile, (t + 1) * tile)
            q = scaled(qg_ref[rows, cols], TOP / pq)
            g = scaled(qg_ref[rows, gcols], TOP / pg)
            s = mxu(kb[:, cols], q, NT) * score_scale
            m = jnp.max(s, axis=0, keepdims=True)
            e = jnp.exp(s - m)
            total = jnp.sum(e, axis=0, keepdims=True)
            o = mxu(vb[:, cols], e.astype(BF16), TN) / total
            d = jnp.sum(o * g.T.astype(F32), axis=0, keepdims=True)
            o_ref[rows, cols] = o.astype(BF16).T
            lse = m + jnp.log(total)
            for p in range(st_ref.shape[0]):
                st_ref[p, 2 * h : 2 * h + 1, rows] = lse
                st_ref[p, 2 * h + 1 : 2 * h + 2, rows] = d


def backward_kernel(heads, tile, qg_ref, kv0, kv1, kv2, kv3, pk_ref, st_ref, dq_ref, dk_ref, dv_ref, kb, vb):
    pk = peak_lanes(pk_ref)
    pq, pkk, pv, pg = (pk[:, i : i + 1] for i in range(4))
    load_keys((kv0, kv1, kv2, kv3), kb, vb, TOP / pkk, TOP / pv)
    score_scale = pq * pkk / (TOP * TOP * ROOT)
    grad_scale = pg * pv / (TOP * TOP)
    width = heads * HD
    for h in range(heads):
        cols = slice(h * HD, (h + 1) * HD)
        gcols = slice(width + h * HD, width + (h + 1) * HD)
        lse = st_ref[:, 2 * h, :]
        top = jnp.max(lse, axis=0, keepdims=True)
        log_total = top + jnp.log(jnp.sum(jnp.exp(lse - top), axis=0, keepdims=True))
        delta = jnp.sum(jnp.exp(lse - log_total) * st_ref[:, 2 * h + 1, :], axis=0, keepdims=True)
        delta = delta * grad_scale
        dk = jnp.zeros((kb.shape[0], HD), F32)
        dv = jnp.zeros((kb.shape[0], HD), F32)
        for t in range(qg_ref.shape[0] // tile):
            rows = slice(t * tile, (t + 1) * tile)
            q = scaled(qg_ref[rows, cols], TOP / pq)
            g = scaled(qg_ref[rows, gcols], TOP / pg)
            s = mxu(kb[:, cols], q, NT) * score_scale
            p = jnp.exp(s - log_total[:, rows])
            dv = dv + mxu(p.astype(BF16), g, NN)
            dp = mxu(vb[:, cols], g, NT) * grad_scale
            ds = (p * (dp - delta[:, rows])).astype(BF16)
            dk = dk + mxu(ds, q, NN)
            dq = mxu(kb[:, cols], ds, TN) * (pkk / (TOP * ROOT))
            dq_ref[rows, cols] = dq.astype(BF16).T
        dk_ref[:, cols] = (dk * (pq / (TOP * ROOT))).astype(BF16)
        dv_ref[:, cols] = (dv * (pg / TOP)).astype(BF16)


def attended_kernel(heads, o_ref, w_ref, pk_ref, out_ref):
    pk = peak_lanes(pk_ref)
    factor = pk[:, 2:3] / TOP
    for h in range(heads):
        cols = slice(h * HD, (h + 1) * HD)
        total = jnp.zeros((o_ref.shape[1], HD), F32)
        for p in range(o_ref.shape[0]):
            total = total + w_ref[p, :, h : h + 1] * o_ref[p, :, cols].astype(F32)
        out_ref[:, cols] = total * factor


def sums_kernel(at_ref, dq_ref, dk0, dk1, dk2, dk3, dv0, dv1, dv2, dv3, gq_ref, gk_ref, gv_ref, pk_ref):
    gq = dq_ref[0].astype(F32)
    for p in range(1, dq_ref.shape[0]):
        gq = gq + dq_ref[p].astype(F32)
    gk = (dk0[...].astype(F32) + dk1[...].astype(F32)) + (dk2[...].astype(F32) + dk3[...].astype(F32))
    gv = (dv0[...].astype(F32) + dv1[...].astype(F32)) + (dv2[...].astype(F32) + dv3[...].astype(F32))
    gq_ref[...] = gq
    gk_ref[...] = gk
    gv_ref[...] = gv
    row = lanes_of([biggest(x) for x in (at_ref[...], gq, gk, gv)])
    pk_ref[...] = jnp.broadcast_to(row[None], pk_ref.shape)


def cast_kernel(at_ref, gq_ref, gk_ref, gv_ref, pk_ref, o0, o1, o2, o3):
    pk = peak_lanes(pk_ref)
    for i, (src, dst) in enumerate(((at_ref, o0), (gq_ref, o1), (gk_ref, o2), (gv_ref, o3))):
        dst[...] = scaled(src[...], TOP / pk[:, i : i + 1])


def shift(n, s):
    return [(i, (i + s) % n) for i in range(n)]


def on_device(sizes, queries, keys, values, out_grad):
    nx, nz, everyone = sizes["x"], sizes["z"], math.prod(sizes.values())
    axes = ("x", "z", "y", "c")
    rows, width = queries.shape
    heads = width // HD
    q_rows, k_rows = rows * nz, rows * nx
    pairs = q_rows * k_rows * heads
    tile = q_rows // 3
    peaks = jax.ShapeDtypeStruct((everyone, 1, 128), F32)
    block = jax.ShapeDtypeStruct((rows, width), F32)
    wide = jax.ShapeDtypeStruct((rows, 2 * width), BF16)

    qg, kv, pk = call(prep_kernel, "prep", (wide, wide, peaks), (queries, keys, values, out_grad), nbytes=2**20)
    kvs = [kv] + [lax.ppermute(kv, "x", shift(nx, s)) for s in range(1, nx)]
    qg_all = lax.all_gather(qg, "z", axis=0, tiled=True)
    pk = lax.all_to_all(pk, axes, 0, 0, tiled=True)

    key_scratch = [pltpu.VMEM((k_rows, width), BF16)] * 2
    o, stats = call(
        functools.partial(forward_kernel, heads, tile),
        "forward",
        (
            jax.ShapeDtypeStruct((q_rows, width), BF16),
            jax.ShapeDtypeStruct((nz, 8, q_rows), F32),
        ),
        (qg_all, *kvs, pk),
        key_scratch,
        flops=4 * pairs * HD,
        nbytes=4 * 2**20,
        exps=pairs,
    )
    stats = lax.all_to_all(stats, "z", 0, 0, tiled=True)
    o = lax.all_to_all(o.reshape(nz, rows, width), "z", 0, 0, tiled=True)
    dq, dk, dv = call(
        functools.partial(backward_kernel, heads, tile),
        "backward",
        (
            jax.ShapeDtypeStruct((q_rows, width), BF16),
            jax.ShapeDtypeStruct((k_rows, width), BF16),
            jax.ShapeDtypeStruct((k_rows, width), BF16),
        ),
        (qg_all, *kvs, pk, stats),
        key_scratch,
        flops=10 * pairs * HD,
        nbytes=6 * 2**20,
        exps=pairs,
    )
    home = lambda d: [d[:rows]] + [
        lax.ppermute(d[s * rows : (s + 1) * rows], "x", shift(nx, nx - s)) for s in range(1, nx)
    ]
    dvs, dks = home(dv), home(dk)
    dq = lax.all_to_all(dq.reshape(nz, rows, width), "z", 0, 0, tiled=True)

    own = lax.dynamic_slice_in_dim(stats, lax.axis_index("z") * rows, rows, 2)[:, 0 : 2 * heads : 2]
    weights = jnp.transpose(jax.nn.softmax(own, axis=0), (0, 2, 1))
    attended = call(functools.partial(attended_kernel, heads), "attended", block, (o, weights, pk), nbytes=2**20)
    gq, gk, gv, tops = call(
        sums_kernel, "sums", (block, block, block, peaks), (attended, dq, *dks, *dvs), nbytes=3 * 2**20
    )
    tops = lax.all_to_all(tops, axes, 0, 0, tiled=True)
    result = jax.ShapeDtypeStruct((rows, width), BF16)
    return call(cast_kernel, "cast", (result,) * 4, (attended, gq, gk, gv, tops), nbytes=2**20)


def solution(mesh):
    sizes = dict(x=4, z=8, y=4, c=2)
    fine = Mesh(mesh.devices.reshape(tuple(sizes.values())), tuple(sizes))
    spec = P(("x", "z"), ("y", "c"))
    return jax.shard_map(
        functools.partial(on_device, sizes),
        mesh=fine,
        in_specs=(spec,) * 4,
        out_specs=(spec,) * 4,
        check_vma=False,
    )
```

```python
import functools
import math

import jax
import jax.numpy as jnp
from jax import lax
from jax.experimental import pallas as pl
from jax.experimental.pallas import tpu as pltpu
from jax.sharding import Mesh
from jax.sharding import PartitionSpec as P

HD = 128
TOP = 4.0
ROOT = math.sqrt(HD)
NT = (((1,), (1,)), ((), ()))
TN = (((0,), (0,)), ((), ()))
NN = (((1,), (0,)), ((), ()))
F32 = jnp.float32
BF16 = jnp.bfloat16
VMEM_LIMIT = 48 * 1024 * 1024
PREP_LIMIT = 62 * 1024 * 1024


def mxu(a, b, dims):
    return lax.dot_general(a, b, dims, preferred_element_type=F32)


def call(body, name, out_shape, args, scratch=(), flops=0, nbytes=0, exps=0, limit=VMEM_LIMIT, **more):
    return pl.pallas_call(
        body,
        name=name,
        out_shape=out_shape,
        scratch_shapes=list(scratch),
        **more,
        compiler_params=pltpu.CompilerParams(vmem_limit_bytes=limit),
        cost_estimate=pl.CostEstimate(flops=flops, bytes_accessed=nbytes, transcendentals=exps),
    )(*args)


def lanes_of(values):
    lane = lax.broadcasted_iota(jnp.int32, (1, 128), 1)
    row = jnp.zeros((1, 128), F32)
    for i, value in enumerate(values):
        row = jnp.where(lane == i, value, row)
    return row


def peak_lanes(ref):
    return jnp.max(ref[...], axis=0)


def biggest(x):
    return jnp.max(jnp.abs(x.astype(F32)), keepdims=True)


def scaled(x, factor):
    return (x.astype(F32) * factor).astype(BF16)


def prep_kernel(q_ref, k_ref, v_ref, g_ref, qg_ref, kv_ref, pk_ref, sems):
    width = q_ref.shape[1]
    left, right = slice(0, width), slice(width, 2 * width)
    places = [(q_ref, qg_ref, left), (k_ref, kv_ref, left), (v_ref, kv_ref, right), (g_ref, qg_ref, right)]
    copies = [
        pltpu.make_async_copy(src, dst.at[:, cols], sems.at[i]) for i, (src, dst, cols) in enumerate(places)
    ]
    for copy in copies:
        copy.start()
    for copy in copies:
        copy.wait()
    row = lanes_of([biggest(dst[:, cols]) for _, dst, cols in places])
    pk_ref[...] = jnp.broadcast_to(row[None], pk_ref.shape)


def place_of(zh, groups, rows, s):
    return pl.ds(pl.multiple_of(lax.rem(zh + groups - s, groups) * rows, 16), rows)


def forward_kernel(heads, groups, wide, zh_ref, *refs):
    qgs, kvs = refs[:groups], refs[groups : groups + wide]
    pk_ref, ot_ref, st_ref, qs, gs, kb, vb = refs[groups + wide :]
    rows, width = qgs[0].shape[0], qs.shape[1]
    span = kvs[0].shape[0]
    pk = peak_lanes(pk_ref)
    pq, pkk, pv, pg = (pk[:, i : i + 1] for i in range(4))
    zh = zh_ref[0]
    for s, ref in enumerate(qgs):
        qs[place_of(zh, groups, rows, s), :] = scaled(ref[:, :width], TOP / pq)
        gs[place_of(zh, groups, rows, s), :] = scaled(ref[:, width:], TOP / pg)
    for s, ref in enumerate(kvs):
        kb[s * span : (s + 1) * span, :] = scaled(ref[:, :width], TOP / pkk)
        vb[s * span : (s + 1) * span, :] = scaled(ref[:, width:], TOP / pv)
    score_scale = pq * pkk / (TOP * TOP * ROOT)
    rows_out = []
    for h in range(heads):
        cols = slice(h * HD, (h + 1) * HD)
        s = mxu(kb[:, cols], qs[:, cols], NT) * score_scale
        m = jnp.max(s, axis=0, keepdims=True)
        e = jnp.exp(s - m)
        total = jnp.sum(e, axis=0, keepdims=True)
        o = mxu(vb[:, cols], e.astype(BF16), TN) / total
        ot_ref[cols, :] = o
        rows_out.append(m + jnp.log(total))
        rows_out.append(jnp.sum(o * gs[:, cols].T.astype(F32), axis=0, keepdims=True))
    for p in range(groups):
        for i, row in enumerate(rows_out):
            st_ref[p, i : i + 1, :] = row
        st_ref[p, len(rows_out) :, :] = jnp.zeros_like(st_ref[p, len(rows_out) :, :])


def backward_kernel(heads, groups, zh_ref, own_ref, st_ref, pk_ref, ot_ref, qs, gs, kb, vb, *refs):
    oqs, dkvs, (oqa,) = refs[:groups], refs[groups : 2 * groups], refs[2 * groups :]
    rows, width = oqs[0].shape[0], qs.shape[1]
    pk = peak_lanes(pk_ref)
    pq, pkk, pv, pg = (pk[:, i : i + 1] for i in range(4))
    score_scale = pq * pkk / (TOP * TOP * ROOT)
    grad_scale = pg * pv / (TOP * TOP)
    zh = zh_ref[0]
    span = kb.shape[0] // groups
    for h in range(heads):
        cols = slice(h * HD, (h + 1) * HD)
        right = slice(width + h * HD, width + (h + 1) * HD)
        lse = st_ref[:, 2 * h, :]
        top = jnp.max(lse, axis=0, keepdims=True)
        log_total = top + jnp.log(jnp.sum(jnp.exp(lse - top), axis=0, keepdims=True))
        delta = jnp.sum(jnp.exp(lse - log_total) * st_ref[:, 2 * h + 1, :], axis=0, keepdims=True)
        delta = delta * grad_scale
        weight = jnp.exp(own_ref[0, 2 * h : 2 * h + 1, :] - log_total) * (pv / TOP)
        oqa[:, cols] = (ot_ref[cols, :] * weight).astype(BF16).T
        q, g, k = qs[:, cols], gs[:, cols], kb[:, cols]
        p = jnp.exp(mxu(k, q, NT) * score_scale - log_total)
        dv = mxu(p.astype(BF16), g, NN) * (pg / TOP)
        dp = mxu(vb[:, cols], g, NT) * grad_scale
        ds = (p * (dp - delta)).astype(BF16)
        dk = mxu(ds, q, NN) * (pq / (TOP * ROOT))
        dq = mxu(k, ds, TN) * (pkk / (TOP * ROOT))
        oqa[:, right] = dq.astype(BF16).T
        for s, ref in enumerate(dkvs):
            part = slice(s * span, (s + 1) * span)
            ref[:, cols] = dk[part].astype(BF16)
            ref[:, right] = dv[part].astype(BF16)
    for s, ref in enumerate(oqs):
        ref[...] = oqa[place_of(zh, groups, rows, s), :]


def fold_kernel(*refs):
    parts, (own_ref, send_ref) = refs[:-2], refs[-2:]
    rows = own_ref.shape[0]
    own_ref[...] = sum(r[:rows, :].astype(F32) for r in parts)
    send_ref[...] = sum(r[rows:, :].astype(F32) for r in parts).astype(BF16)


def sums_kernel(groups, own_ref, got_ref, *refs):
    oqs, (goq_ref, gkv_ref, pk_ref) = refs[:groups], refs[groups:]
    width = own_ref.shape[1] // 2
    goq_ref[...] = sum(r[...].astype(F32) for r in oqs)
    gkv_ref[...] = own_ref[...] + got_ref[...].astype(F32)
    row = lanes_of([biggest(r[:, c]) for r in (goq_ref, gkv_ref) for c in (slice(0, width), slice(width, 2 * width))])
    pk_ref[...] = jnp.broadcast_to(row[None], pk_ref.shape)


def cast_kernel(goq_ref, gkv_ref, pk_ref, *outs):
    pk = peak_lanes(pk_ref)
    width = outs[0].shape[1]
    sources = [r[:, c] for r in (goq_ref, gkv_ref) for c in (slice(0, width), slice(width, 2 * width))]
    for i, (src, dst) in enumerate(zip(sources, outs)):
        dst[...] = scaled(src, TOP / pk[:, i : i + 1])


def shift(n, s):
    return [(i, (i + s) % n) for i in range(n)]


def spread(x, axis, n):
    return [x] + [lax.ppermute(x, axis, shift(n, s)) for s in range(1, n)]


def home(parts, axis):
    n = len(parts)
    return [parts[0]] + [lax.ppermute(parts[s], axis, shift(n, n - s)) for s in range(1, n)]


def like(dtype, *shape):
    return jax.ShapeDtypeStruct(shape, dtype)


def on_device(sizes, queries, keys, values, out_grad):
    groups, everyone = sizes["zh"], math.prod(sizes.values())
    axes = tuple(sizes)
    rows, width = queries.shape
    heads = width // HD
    q_rows, k_rows = rows * groups, rows * sizes["x"] * sizes["zl"]
    pairs = q_rows * k_rows * heads
    peaks = like(F32, everyone, 1, 128)
    wide = like(BF16, rows, 2 * width)
    zh = lax.axis_index("zh").astype(jnp.int32).reshape(1)
    smem = pl.BlockSpec(memory_space=pltpu.SMEM)
    vmem = pl.BlockSpec(memory_space=pltpu.VMEM)
    hbm = pl.BlockSpec(memory_space=pltpu.HBM)

    qg, kv, pk = call(
        prep_kernel,
        "prep",
        (wide, wide, peaks),
        (queries, keys, values, out_grad),
        [pltpu.SemaphoreType.DMA((4,))],
        nbytes=2**20,
        limit=PREP_LIMIT,
        in_specs=[hbm] * 4,
    )
    twin = lax.ppermute(kv, "zl", shift(2, 1))
    near = spread(kv, "x", sizes["x"])
    qgs = spread(qg, "zh", groups)
    far = spread(twin, "x", sizes["x"])
    pk = lax.all_to_all(pk, axes, 0, 0, tiled=True)
    kvs = [one for two in zip(near, far) for one in two]

    ot, stats, qs, gs, kb, vb = call(
        functools.partial(forward_kernel, heads, groups, len(kvs)),
        "forward",
        (like(F32, width, q_rows), like(F32, groups, 8, q_rows))
        + (like(BF16, q_rows, width),) * 2
        + (like(BF16, k_rows, width),) * 2,
        (zh, *qgs, *kvs, pk),
        flops=4 * pairs * HD,
        nbytes=4 * 2**20,
        exps=pairs,
        in_specs=[smem] + [vmem] * (groups + len(kvs) + 1),
    )
    sts = lax.all_to_all(stats, "zh", 0, 0, tiled=True)
    outs = call(
        functools.partial(backward_kernel, heads, groups),
        "backward",
        (wide,) * groups + (like(BF16, k_rows // groups, 2 * width),) * groups,
        (zh, stats, sts, pk, ot, qs, gs, kb, vb),
        [pltpu.VMEM((q_rows, 2 * width), BF16)],
        flops=10 * pairs * HD,
        nbytes=6 * 2**20,
        exps=pairs,
        in_specs=[smem] + [vmem] * 8,
    )
    dkvs = home(outs[groups:], "x")
    oqs = home(outs[:groups], "zh")
    own, send = call(fold_kernel, "fold", (like(F32, rows, 2 * width), wide), dkvs, nbytes=2 * 2**20)
    got = lax.ppermute(send, "zl", shift(2, 1))
    goq, gkv, tops = call(
        functools.partial(sums_kernel, groups),
        "sums",
        (like(F32, rows, 2 * width), like(F32, rows, 2 * width), peaks),
        (own, got, *oqs),
        nbytes=3 * 2**20,
    )
    tops = lax.all_to_all(tops, axes, 0, 0, tiled=True)
    return call(cast_kernel, "cast", (like(BF16, rows, width),) * 4, (goq, gkv, tops), nbytes=2**20)


def solution(mesh):
    sizes = dict(x=4, zh=4, zl=2, y=4, c=2)
    fine = Mesh(mesh.devices.reshape(tuple(sizes.values())), tuple(sizes))
    spec = P(("x", "zh", "zl"), ("y", "c"))
    return jax.shard_map(
        functools.partial(on_device, sizes),
        mesh=fine,
        in_specs=(spec,) * 4,
        out_specs=(spec,) * 4,
        check_vma=False,
    )
```

```python
import functools
import math

import jax
import jax.numpy as jnp
from jax import lax
from jax.experimental import pallas as pl
from jax.experimental.pallas import tpu as pltpu
from jax.sharding import Mesh
from jax.sharding import PartitionSpec as P

HD = 128
TOP = 4.0
ROOT = math.sqrt(HD)
NT = (((1,), (1,)), ((), ()))
TN = (((0,), (0,)), ((), ()))
NN = (((1,), (0,)), ((), ()))
F32 = jnp.float32
BF16 = jnp.bfloat16
VMEM_LIMIT = 48 * 1024 * 1024
WORK_LIMIT = 24 * 1024 * 1024
FORWARD_LIMIT = 32 * 1024 * 1024
PREP_LIMIT = 62 * 1024 * 1024


def mxu(a, b, dims):
    return lax.dot_general(a, b, dims, preferred_element_type=F32)


def call(body, name, out_shape, args, scratch=(), flops=0, nbytes=0, exps=0, limit=VMEM_LIMIT, **more):
    return pl.pallas_call(
        body,
        name=name,
        out_shape=out_shape,
        scratch_shapes=list(scratch),
        **more,
        compiler_params=pltpu.CompilerParams(vmem_limit_bytes=limit),
        cost_estimate=pl.CostEstimate(flops=flops, bytes_accessed=nbytes, transcendentals=exps),
    )(*args)


def lanes_of(values):
    lane = lax.broadcasted_iota(jnp.int32, (1, 128), 1)
    row = jnp.zeros((1, 128), F32)
    for i, value in enumerate(values):
        row = jnp.where(lane == i, value, row)
    return row


def peak_lanes(ref):
    return jnp.max(ref[...], axis=0)


def biggest(x):
    return jnp.max(jnp.abs(x.astype(F32)), keepdims=True)


def scaled(x, factor):
    return (x.astype(F32) * factor).astype(BF16)


def prep_kernel(q_ref, k_ref, v_ref, g_ref, qg_ref, kv_ref, pk_ref, sems):
    width = q_ref.shape[1]
    left, right = slice(0, width), slice(width, 2 * width)
    places = [(q_ref, qg_ref, left), (k_ref, kv_ref, left), (v_ref, kv_ref, right), (g_ref, qg_ref, right)]
    copies = [
        pltpu.make_async_copy(src, dst.at[:, cols], sems.at[i]) for i, (src, dst, cols) in enumerate(places)
    ]
    for copy in copies:
        copy.start()
    for copy in copies:
        copy.wait()
    row = lanes_of([biggest(dst[:, cols]) for _, dst, cols in places])
    pk_ref[...] = jnp.broadcast_to(row[None], pk_ref.shape)


def place_of(zh, groups, rows, s):
    return pl.ds(pl.multiple_of(lax.rem(zh + groups - s, groups) * rows, 16), rows)


def forward_kernel(heads, groups, shards, zh_ref, *refs):
    qgs, kvs = refs[:groups], refs[groups : groups + shards]
    pk_ref, e_ref, ot_ref, row_ref, st_ref, qs, gs, kb, vb = refs[groups + shards :]
    rows, width = qgs[0].shape[0], qs.shape[1]
    pk = peak_lanes(pk_ref)
    pq, pkk, pv, pg = (pk[:, i : i + 1] for i in range(4))
    zh = zh_ref[0]
    for s, ref in enumerate(qgs):
        qs[place_of(zh, groups, rows, s), :] = scaled(ref[:, :width], TOP / pq)
        gs[place_of(zh, groups, rows, s), :] = scaled(ref[:, width:], TOP / pg)
    for s, ref in enumerate(kvs):
        kb[s * rows : (s + 1) * rows, :] = scaled(ref[:, :width], TOP / pkk)
        vb[s * rows : (s + 1) * rows, :] = scaled(ref[:, width:], TOP / pv)
    score_scale = pq * pkk / (TOP * TOP * ROOT)
    st_ref[...] = jnp.zeros_like(st_ref)
    row_ref[...] = jnp.zeros_like(row_ref)
    for h in range(heads):
        cols = slice(h * HD, (h + 1) * HD)
        s = mxu(kb[:, cols], qs[:, cols], NT) * score_scale
        m = jnp.max(s, axis=0, keepdims=True)
        e = jnp.exp(s - m)
        e_ref[h] = e
        total = jnp.sum(e, axis=0, keepdims=True)
        o = mxu(vb[:, cols], e.astype(BF16), TN) / total
        ot_ref[cols, :] = o
        row_ref[h : h + 1, :] = m
        st_ref[2 * h : 2 * h + 1, :] = m + jnp.log(total)
        st_ref[2 * h + 1 : 2 * h + 2, :] = jnp.sum(o * gs[:, cols].T.astype(F32), axis=0, keepdims=True)


def middle_kernel(heads, gs, vb, dp):
    for h in range(heads):
        cols = slice(h * HD, (h + 1) * HD)
        dp[h] = mxu(vb[:, cols], gs[:, cols], NT)


def totals(sts, h):
    lses = [st[2 * h : 2 * h + 1, :] for st in sts]
    top = functools.reduce(jnp.maximum, lses)
    log_total = top + jnp.log(sum(jnp.exp(x - top) for x in lses))
    delta = sum(jnp.exp(x - log_total) * st[2 * h + 1 : 2 * h + 2, :] for x, st in zip(lses, sts))
    return log_total, delta


def keys_kernel(heads, groups, *refs):
    sts, (pk_ref, qs, gs, e, row_ref, dp, ds), dkvs = refs[:groups], refs[groups : groups + 7], refs[groups + 7 :]
    pk = peak_lanes(pk_ref)
    pq, pkk, pv, pg = (pk[:, i : i + 1] for i in range(4))
    grad_scale = pg * pv / (TOP * TOP)
    width = qs.shape[1]
    span = e.shape[1] // groups
    for h in range(heads):
        left = slice(h * HD, (h + 1) * HD)
        right = slice(width + h * HD, width + (h + 1) * HD)
        log_total, delta = totals(sts, h)
        p = e[h] * jnp.exp(row_ref[h : h + 1, :] - log_total)
        dv = mxu(p.astype(BF16), gs[:, left], NN) * (pg / TOP)
        d = (p * (dp[h] * grad_scale - delta * grad_scale)).astype(BF16)
        ds[h] = d
        dk = mxu(d, qs[:, left], NN) * (pq / (TOP * ROOT))
        for s, ref in enumerate(dkvs):
            part = slice(s * span, (s + 1) * span)
            ref[:, left] = dk[part].astype(BF16)
            ref[:, right] = dv[part].astype(BF16)


def queries_kernel(heads, groups, zh_ref, *refs):
    sts, (pk_ref, ot_ref, kb, ds) = refs[:groups], refs[groups : groups + 4]
    oqs, oqa = refs[groups + 4 : -1], refs[-1]
    rows, width = oqs[0].shape[0], kb.shape[1]
    pk = peak_lanes(pk_ref)
    for h in range(heads):
        left = slice(h * HD, (h + 1) * HD)
        right = slice(width + h * HD, width + (h + 1) * HD)
        log_total, _ = totals(sts, h)
        weight = jnp.exp(sts[0][2 * h : 2 * h + 1, :] - log_total) * (pk[:, 2:3] / TOP)
        oqa[:, left] = (ot_ref[left, :] * weight).astype(BF16).T
        dq = mxu(kb[:, left], ds[h], TN) * (pk[:, 1:2] / (TOP * ROOT))
        oqa[:, right] = dq.astype(BF16).T
    for s, ref in enumerate(oqs):
        ref[...] = oqa[place_of(zh_ref[0], groups, rows, s), :]


def fold_kernel(*refs):
    parts, (own_ref, send_ref) = refs[:-2], refs[-2:]
    rows = own_ref.shape[0]
    own_ref[...] = sum(r[:rows, :].astype(F32) for r in parts)
    send_ref[...] = sum(r[rows:, :].astype(F32) for r in parts).astype(BF16)


def sums_kernel(groups, own_ref, got_ref, *refs):
    oqs, (goq_ref, gkv_ref, pk_ref) = refs[:groups], refs[groups:]
    width = own_ref.shape[1] // 2
    goq_ref[...] = sum(r[...].astype(F32) for r in oqs)
    gkv_ref[...] = own_ref[...] + got_ref[...].astype(F32)
    row = lanes_of([biggest(r[:, c]) for r in (goq_ref, gkv_ref) for c in (slice(0, width), slice(width, 2 * width))])
    pk_ref[...] = jnp.broadcast_to(row[None], pk_ref.shape)


def cast_kernel(goq_ref, gkv_ref, pk_ref, *outs):
    pk = peak_lanes(pk_ref)
    width = outs[0].shape[1]
    sources = [r[:, c] for r in (goq_ref, gkv_ref) for c in (slice(0, width), slice(width, 2 * width))]
    for i, (src, dst) in enumerate(zip(sources, outs)):
        dst[...] = scaled(src, TOP / pk[:, i : i + 1])


def shift(n, s):
    return [(i, (i + s) % n) for i in range(n)]


def spread(x, axis, n):
    return [x] + [lax.ppermute(x, axis, shift(n, s)) for s in range(1, n)]


def home(parts, axis):
    n = len(parts)
    return [parts[0]] + [lax.ppermute(parts[s], axis, shift(n, n - s)) for s in range(1, n)]


def like(dtype, *shape):
    return jax.ShapeDtypeStruct(shape, dtype)


def on_device(sizes, queries, keys, values, out_grad):
    groups, everyone = sizes["zh"], math.prod(sizes.values())
    axes = tuple(sizes)
    rows, width = queries.shape
    heads = width // HD
    q_rows, k_rows = rows * groups, rows * sizes["x"] * sizes["zl"]
    pairs = q_rows * k_rows * heads
    peaks = like(F32, everyone, 1, 128)
    wide = like(BF16, rows, 2 * width)
    zh = lax.axis_index("zh").astype(jnp.int32).reshape(1)
    smem = pl.BlockSpec(memory_space=pltpu.SMEM)
    vmem = pl.BlockSpec(memory_space=pltpu.VMEM)
    hbm = pl.BlockSpec(memory_space=pltpu.HBM)

    qg, kv, pk = call(
        prep_kernel,
        "prep",
        (wide, wide, peaks),
        (queries, keys, values, out_grad),
        [pltpu.SemaphoreType.DMA((4,))],
        nbytes=2**20,
        limit=PREP_LIMIT,
        in_specs=[hbm] * 4,
    )
    twin = lax.ppermute(kv, "zl", shift(2, 1))
    near = spread(kv, "x", sizes["x"])
    qgs = spread(qg, "zh", groups)
    far = spread(twin, "x", sizes["x"])
    pk = lax.all_to_all(pk, axes, 0, 0, tiled=True)
    kvs = [one for two in zip(near, far) for one in two]

    square = like(F32, heads, k_rows, q_rows)
    some_rows = like(F32, 8, q_rows)
    e, ot, top, stats, qs, gs, kb, vb = call(
        functools.partial(forward_kernel, heads, groups, len(kvs)),
        "forward",
        (square, like(F32, width, q_rows), some_rows, some_rows)
        + (like(BF16, q_rows, width),) * 2
        + (like(BF16, k_rows, width),) * 2,
        (zh, *qgs, *kvs, pk),
        flops=4 * pairs * HD,
        nbytes=4 * 2**20,
        exps=pairs,
        limit=FORWARD_LIMIT,
        in_specs=[smem] + [vmem] * (groups + len(kvs) + 1),
    )
    sts = home([stats] * groups, "zh")
    dp = call(
        functools.partial(middle_kernel, heads),
        "middle",
        square,
        (gs, vb),
        flops=2 * pairs * HD,
        nbytes=8 * 2**20,
        limit=WORK_LIMIT,
    )
    ds, *dkvs = call(
        functools.partial(keys_kernel, heads, groups),
        "keys",
        (like(BF16, heads, k_rows, q_rows),) + (like(BF16, k_rows // groups, 2 * width),) * groups,
        (*sts, pk, qs, gs, e, top, dp),
        flops=4 * pairs * HD,
        nbytes=6 * 2**20,
        limit=WORK_LIMIT,
    )
    oqs = call(
        functools.partial(queries_kernel, heads, groups),
        "queries",
        (wide,) * groups,
        (zh, *sts, pk, ot, kb, ds),
        [pltpu.VMEM((q_rows, 2 * width), BF16)],
        flops=2 * pairs * HD,
        nbytes=6 * 2**20,
        limit=WORK_LIMIT,
        in_specs=[smem] + [vmem] * (groups + 4),
    )
    dkvs = home(dkvs, "x")
    oqs = home(oqs, "zh")
    own, send = call(fold_kernel, "fold", (like(F32, rows, 2 * width), wide), dkvs, nbytes=2 * 2**20)
    got = lax.ppermute(send, "zl", shift(2, 1))
    goq, gkv, tops = call(
        functools.partial(sums_kernel, groups),
        "sums",
        (like(F32, rows, 2 * width), like(F32, rows, 2 * width), peaks),
        (own, got, *oqs),
        nbytes=3 * 2**20,
    )
    tops = lax.all_to_all(tops, axes, 0, 0, tiled=True)
    return call(cast_kernel, "cast", (like(BF16, rows, width),) * 4, (goq, gkv, tops), nbytes=2**20)


def solution(mesh):
    sizes = dict(x=4, zh=4, zl=2, y=4, c=2)
    fine = Mesh(mesh.devices.reshape(tuple(sizes.values())), tuple(sizes))
    spec = P(("x", "zh", "zl"), ("y", "c"))
    return jax.shard_map(
        functools.partial(on_device, sizes),
        mesh=fine,
        in_specs=(spec,) * 4,
        out_specs=(spec,) * 4,
        check_vma=False,
    )
```

```python
import functools
import math

import jax
import jax.numpy as jnp
from jax import lax
from jax.experimental import pallas as pl
from jax.experimental.pallas import tpu as pltpu
from jax.sharding import Mesh
from jax.sharding import PartitionSpec as P

HD = 128
TOP = 4.0
ROOT = math.sqrt(HD)
NT = (((1,), (1,)), ((), ()))
TN = (((0,), (0,)), ((), ()))
NN = (((1,), (0,)), ((), ()))
F32 = jnp.float32
BF16 = jnp.bfloat16
VMEM_LIMIT = 48 * 1024 * 1024
WORK_LIMIT = 24 * 1024 * 1024
FORWARD_LIMIT = 32 * 1024 * 1024
PREP_LIMIT = 62 * 1024 * 1024


def mxu(a, b, dims):
    return lax.dot_general(a, b, dims, preferred_element_type=F32)


def call(body, name, out_shape, args, scratch=(), flops=0, nbytes=0, exps=0, limit=VMEM_LIMIT, **more):
    return pl.pallas_call(
        body,
        name=name,
        out_shape=out_shape,
        scratch_shapes=list(scratch),
        **more,
        compiler_params=pltpu.CompilerParams(vmem_limit_bytes=limit),
        cost_estimate=pl.CostEstimate(flops=flops, bytes_accessed=nbytes, transcendentals=exps),
    )(*args)


def lanes_of(values):
    lane = lax.broadcasted_iota(jnp.int32, (1, 128), 1)
    row = jnp.zeros((1, 128), F32)
    for i, value in enumerate(values):
        row = jnp.where(lane == i, value, row)
    return row


def peak_lanes(ref):
    return jnp.max(ref[...], axis=0)


def biggest(x):
    return jnp.max(jnp.abs(x.astype(F32)), keepdims=True)


def scaled(x, factor):
    return (x.astype(F32) * factor).astype(BF16)


def prep_kernel(q_ref, k_ref, v_ref, g_ref, qg_ref, kv_ref, pk_ref, sems):
    width = q_ref.shape[1]
    left, right = slice(0, width), slice(width, 2 * width)
    places = [(q_ref, qg_ref, left), (k_ref, kv_ref, left), (v_ref, kv_ref, right), (g_ref, qg_ref, right)]
    copies = [
        pltpu.make_async_copy(src, dst.at[:, cols], sems.at[i]) for i, (src, dst, cols) in enumerate(places)
    ]
    for copy in copies:
        copy.start()
    for copy in copies:
        copy.wait()
    row = lanes_of([biggest(dst[:, cols]) for _, dst, cols in places])
    pk_ref[...] = jnp.broadcast_to(row[None], pk_ref.shape)


def place_of(zh, groups, rows, s):
    return pl.ds(pl.multiple_of(lax.rem(zh + groups - s, groups) * rows, 16), rows)


def half_pass(heads, pk, qs, gs, kb, vb, e_ref):
    pq, pkk = pk[:, 0:1], pk[:, 1:2]
    score_scale = pq * pkk / (TOP * TOP * ROOT)
    to_power = score_scale * math.log2(math.e)
    found = []
    for h in range(heads):
        cols = slice(h * HD, (h + 1) * HD)
        s = mxu(kb[:, cols], qs[:, cols], NT)
        peak = jnp.max(s, axis=0, keepdims=True)
        e = jnp.exp2(s * to_power - peak * to_power)
        m = peak * score_scale
        e_ref[h] = e
        total = jnp.sum(e, axis=0, keepdims=True)
        o = mxu(vb[:, cols], e.astype(BF16), TN) / total
        d = jnp.sum(o * gs[:, cols].T.astype(F32), axis=0, keepdims=True)
        found.append((m, m + jnp.log(total), d, o))
    return found


def load_keys(parts, pk, kb, vb):
    rows, width = parts[0].shape[0], kb.shape[1]
    for s, ref in enumerate(parts):
        kb[s * rows : (s + 1) * rows, :] = scaled(ref[:, :width], TOP / pk[:, 1:2])
        vb[s * rows : (s + 1) * rows, :] = scaled(ref[:, width:], TOP / pk[:, 2:3])


def near_kernel(heads, groups, zh_ref, *refs):
    qgs, near = refs[:groups], refs[groups : 2 * groups]
    pk_ref, qs, gs, kb, vb, e_ref, ot_ref, row_ref = refs[2 * groups :]
    rows, width = qgs[0].shape[0], qs.shape[1]
    pk = peak_lanes(pk_ref)
    zh = zh_ref[0]
    for s, ref in enumerate(qgs):
        qs[place_of(zh, groups, rows, s), :] = scaled(ref[:, :width], TOP / pk[:, 0:1])
        gs[place_of(zh, groups, rows, s), :] = scaled(ref[:, width:], TOP / pk[:, 3:4])
    load_keys(near, pk, kb, vb)
    row_ref[...] = jnp.zeros_like(row_ref)
    for h, (m, lse, d, o) in enumerate(half_pass(heads, pk, qs, gs, kb, vb, e_ref)):
        ot_ref[h * HD : (h + 1) * HD, :] = o
        for i, row in enumerate((m, lse, d)):
            row_ref[3 * h + i : 3 * h + i + 1, :] = row


def far_kernel(heads, groups, *refs):
    far = refs[:groups]
    pk_ref, qs, gs, ot1_ref, row1_ref, kb, vb, e_ref, ot_ref, row_ref, st_ref = refs[groups:]
    pk = peak_lanes(pk_ref)
    load_keys(far, pk, kb, vb)
    row_ref[...] = jnp.zeros_like(row_ref)
    stats = []
    for h, (m, lse, d, o) in enumerate(half_pass(heads, pk, qs, gs, kb, vb, e_ref)):
        cols = slice(h * HD, (h + 1) * HD)
        lse1, d1 = (row1_ref[3 * h + i : 3 * h + i + 1, :] for i in (1, 2))
        top = jnp.maximum(lse, lse1)
        both = top + jnp.log(jnp.exp(lse - top) + jnp.exp(lse1 - top))
        w, w1 = jnp.exp(lse - both), jnp.exp(lse1 - both)
        ot_ref[cols, :] = w * o + w1 * ot1_ref[cols, :]
        row_ref[h : h + 1, :] = m
        stats += [both, w * d + w1 * d1]
    st_ref[...] = jnp.zeros_like(st_ref)
    for i, row in enumerate(stats):
        st_ref[i : i + 1, :] = row


def middle_kernel(heads, gs, vb1, vb2, dp1, dp2):
    for h in range(heads):
        cols = slice(h * HD, (h + 1) * HD)
        for vb, dp in ((vb1, dp1), (vb2, dp2)):
            dp[h] = mxu(vb[:, cols], gs[:, cols], NT)


def totals(sts, h):
    lses = [st[2 * h : 2 * h + 1, :] for st in sts]
    top = functools.reduce(jnp.maximum, lses)
    log_total = top + jnp.log(sum(jnp.exp(x - top) for x in lses))
    delta = sum(jnp.exp(x - log_total) * st[2 * h + 1 : 2 * h + 2, :] for x, st in zip(lses, sts))
    return log_total, delta


def keys_kernel(heads, groups, *refs):
    sts, dkvs = refs[:groups], refs[-groups:]
    pk_ref, qs, gs, e1, e2, row1_ref, row2_ref, dp1, dp2, ds1, ds2 = refs[groups:-groups]
    pk = peak_lanes(pk_ref)
    pq, pkk, pv, pg = (pk[:, i : i + 1] for i in range(4))
    grad_scale = pg * pv / (TOP * TOP)
    width = qs.shape[1]
    rows = e1.shape[1] // groups
    for h in range(heads):
        left = slice(h * HD, (h + 1) * HD)
        right = slice(width + h * HD, width + (h + 1) * HD)
        log_total, delta = totals(sts, h)
        delta = delta * grad_scale
        q, g = qs[:, left], gs[:, left]
        halves = ((e1, row1_ref[3 * h : 3 * h + 1, :], dp1, ds1), (e2, row2_ref[h : h + 1, :], dp2, ds2))
        for half, (e, m, dp, ds) in enumerate(halves):
            p = e[h] * jnp.exp(m - log_total)
            dv = mxu(p.astype(BF16), g, NN) * (pg / TOP)
            d = (p * (dp[h] * grad_scale - delta)).astype(BF16)
            ds[h] = d
            dk = mxu(d, q, NN) * (pq / (TOP * ROOT))
            for s, ref in enumerate(dkvs):
                part, to = slice(s * rows, (s + 1) * rows), slice(half * rows, (half + 1) * rows)
                ref[to, left] = dk[part].astype(BF16)
                ref[to, right] = dv[part].astype(BF16)


def queries_kernel(heads, groups, zh_ref, *refs):
    sts, (pk_ref, ot_ref, kb1, kb2, ds1, ds2) = refs[:groups], refs[groups : groups + 6]
    oqs, oqa = refs[groups + 6 : -1], refs[-1]
    rows, width = oqs[0].shape[0], kb1.shape[1]
    pk = peak_lanes(pk_ref)
    for h in range(heads):
        left = slice(h * HD, (h + 1) * HD)
        right = slice(width + h * HD, width + (h + 1) * HD)
        log_total, _ = totals(sts, h)
        weight = jnp.exp(sts[0][2 * h : 2 * h + 1, :] - log_total) * (pk[:, 2:3] / TOP)
        oqa[:, left] = (ot_ref[left, :] * weight).astype(BF16).T
        dq = mxu(kb1[:, left], ds1[h], TN) + mxu(kb2[:, left], ds2[h], TN)
        dq = dq * (pk[:, 1:2] / (TOP * ROOT))
        oqa[:, right] = dq.astype(BF16).T
    for s, ref in enumerate(oqs):
        ref[...] = oqa[place_of(zh_ref[0], groups, rows, s), :]


def fold_kernel(*refs):
    parts, (own_ref, send_ref) = refs[:-2], refs[-2:]
    rows = own_ref.shape[0]
    own_ref[...] = sum(r[:rows, :].astype(F32) for r in parts)
    send_ref[...] = sum(r[rows:, :].astype(F32) for r in parts).astype(BF16)


def sums_kernel(groups, own_ref, got_ref, *refs):
    oqs, (goq_ref, gkv_ref, pk_ref) = refs[:groups], refs[groups:]
    width = own_ref.shape[1] // 2
    goq_ref[...] = sum(r[...].astype(F32) for r in oqs)
    gkv_ref[...] = own_ref[...] + got_ref[...].astype(F32)
    row = lanes_of([biggest(r[:, c]) for r in (goq_ref, gkv_ref) for c in (slice(0, width), slice(width, 2 * width))])
    pk_ref[...] = jnp.broadcast_to(row[None], pk_ref.shape)


def cast_kernel(goq_ref, gkv_ref, pk_ref, *outs):
    pk = peak_lanes(pk_ref)
    width = outs[0].shape[1]
    sources = [r[:, c] for r in (goq_ref, gkv_ref) for c in (slice(0, width), slice(width, 2 * width))]
    for i, (src, dst) in enumerate(zip(sources, outs)):
        dst[...] = scaled(src, TOP / pk[:, i : i + 1])


def shift(n, s):
    return [(i, (i + s) % n) for i in range(n)]


def spread(x, axis, n):
    return [x] + [lax.ppermute(x, axis, shift(n, s)) for s in range(1, n)]


def home(parts, axis):
    n = len(parts)
    return [parts[0]] + [lax.ppermute(parts[s], axis, shift(n, n - s)) for s in range(1, n)]


def like(dtype, *shape):
    return jax.ShapeDtypeStruct(shape, dtype)


def on_device(sizes, queries, keys, values, out_grad):
    groups, everyone = sizes["zh"], math.prod(sizes.values())
    axes = tuple(sizes)
    rows, width = queries.shape
    heads = width // HD
    q_rows, k_rows = rows * groups, rows * sizes["x"] * sizes["zl"]
    pairs = q_rows * k_rows * heads
    peaks = like(F32, everyone, 1, 128)
    wide = like(BF16, rows, 2 * width)
    zh = lax.axis_index("zh").astype(jnp.int32).reshape(1)
    smem = pl.BlockSpec(memory_space=pltpu.SMEM)
    vmem = pl.BlockSpec(memory_space=pltpu.VMEM)
    hbm = pl.BlockSpec(memory_space=pltpu.HBM)

    qg, kv, pk = call(
        prep_kernel,
        "prep",
        (wide, wide, peaks),
        (queries, keys, values, out_grad),
        [pltpu.SemaphoreType.DMA((4,))],
        nbytes=2**20,
        limit=PREP_LIMIT,
        in_specs=[hbm] * 4,
    )
    twin = lax.ppermute(kv, "zl", shift(2, 1))
    near = spread(kv, "x", sizes["x"])
    qgs = spread(qg, "zh", groups)
    far = spread(twin, "x", sizes["x"])
    pk = lax.all_to_all(pk, axes, 0, 0, tiled=True)
    half = like(BF16, q_rows, width)
    square = like(F32, heads, q_rows, q_rows)
    some_rows = like(F32, 16, q_rows)
    outputs = like(F32, width, q_rows)
    qs, gs, kb1, vb1, e1, ot1, row1 = call(
        functools.partial(near_kernel, heads, groups),
        "near",
        (half,) * 4 + (square, outputs, some_rows),
        (zh, *qgs, *near, pk),
        flops=2 * pairs * HD,
        nbytes=4 * 2**20,
        exps=pairs // 2,
        limit=FORWARD_LIMIT,
        in_specs=[smem] + [vmem] * (2 * groups + 1),
    )
    kb2, vb2, e2, ot, row2, stats = call(
        functools.partial(far_kernel, heads, groups),
        "far",
        (half,) * 2 + (square, outputs, some_rows, like(F32, 8, q_rows)),
        (*far, pk, qs, gs, ot1, row1),
        flops=2 * pairs * HD,
        nbytes=4 * 2**20,
        exps=pairs // 2,
        limit=FORWARD_LIMIT,
    )
    sts = home([stats] * groups, "zh")
    dp1, dp2 = call(
        functools.partial(middle_kernel, heads),
        "middle",
        (square, square),
        (gs, vb1, vb2),
        flops=2 * pairs * HD,
        nbytes=8 * 2**20,
        limit=WORK_LIMIT,
    )
    edges = like(BF16, heads, q_rows, q_rows)
    ds1, ds2, *dkvs = call(
        functools.partial(keys_kernel, heads, groups),
        "keys",
        (edges, edges) + (like(BF16, 2 * rows, 2 * width),) * groups,
        (*sts, pk, qs, gs, e1, e2, row1, row2, dp1, dp2),
        flops=4 * pairs * HD,
        nbytes=6 * 2**20,
        limit=WORK_LIMIT,
    )
    oqs = call(
        functools.partial(queries_kernel, heads, groups),
        "queries",
        (wide,) * groups,
        (zh, *sts, pk, ot, kb1, kb2, ds1, ds2),
        [pltpu.VMEM((q_rows, 2 * width), BF16)],
        flops=2 * pairs * HD,
        nbytes=6 * 2**20,
        limit=WORK_LIMIT,
        in_specs=[smem] + [vmem] * (groups + 6),
    )
    dkvs = home(dkvs, "x")
    oqs = home(oqs, "zh")
    own, send = call(fold_kernel, "fold", (like(F32, rows, 2 * width), wide), dkvs, nbytes=2 * 2**20)
    got = lax.ppermute(send, "zl", shift(2, 1))
    goq, gkv, tops = call(
        functools.partial(sums_kernel, groups),
        "sums",
        (like(F32, rows, 2 * width), like(F32, rows, 2 * width), peaks),
        (own, got, *oqs),
        nbytes=3 * 2**20,
    )
    tops = lax.all_to_all(tops, axes, 0, 0, tiled=True)
    return call(cast_kernel, "cast", (like(BF16, rows, width),) * 4, (goq, gkv, tops), nbytes=2**20)


def solution(mesh):
    sizes = dict(x=4, zh=4, zl=2, y=4, c=2)
    fine = Mesh(mesh.devices.reshape(tuple(sizes.values())), tuple(sizes))
    spec = P(("x", "zh", "zl"), ("y", "c"))
    return jax.shard_map(
        functools.partial(on_device, sizes),
        mesh=fine,
        in_specs=(spec,) * 4,
        out_specs=(spec,) * 4,
        check_vma=False,
    )
```

```python
import functools
import math

import jax
import jax.numpy as jnp
from jax import lax
from jax.experimental import pallas as pl
from jax.experimental.pallas import tpu as pltpu
from jax.sharding import Mesh
from jax.sharding import PartitionSpec as P

HD = 128
TOP = 4.0
ROOT = math.sqrt(HD)
NT = (((1,), (1,)), ((), ()))
TN = (((0,), (0,)), ((), ()))
NN = (((1,), (0,)), ((), ()))
F32 = jnp.float32
BF16 = jnp.bfloat16
VMEM_LIMIT = 48 * 1024 * 1024
WORK_LIMIT = 24 * 1024 * 1024
PEAK_ROW = 15
FORWARD_LIMIT = 32 * 1024 * 1024
PREP_LIMIT = 62 * 1024 * 1024


def mxu(a, b, dims):
    return lax.dot_general(a, b, dims, preferred_element_type=F32)


def call(body, name, out_shape, args, scratch=(), flops=0, nbytes=0, exps=0, limit=VMEM_LIMIT, **more):
    return pl.pallas_call(
        body,
        name=name,
        out_shape=out_shape,
        scratch_shapes=list(scratch),
        **more,
        compiler_params=pltpu.CompilerParams(vmem_limit_bytes=limit),
        cost_estimate=pl.CostEstimate(flops=flops, bytes_accessed=nbytes, transcendentals=exps),
    )(*args)


def lanes_of(values):
    lane = lax.broadcasted_iota(jnp.int32, (1, 128), 1)
    row = jnp.zeros((1, 128), F32)
    for i, value in enumerate(values):
        row = jnp.where(lane == i, value, row)
    return row


def peak_lanes(ref):
    step = ref.shape[0] // 8
    parts = [jnp.max(ref[i * step : (i + 1) * step], axis=0) for i in range(8)]
    while len(parts) > 1:
        parts = [jnp.maximum(a, b) for a, b in zip(parts[::2], parts[1::2])]
    return parts[0]


def biggest(x):
    return jnp.max(jnp.abs(x.astype(F32)), keepdims=True)


def scaled(x, factor):
    return (x.astype(F32) * factor).astype(BF16)


def prep_kernel(q_ref, k_ref, v_ref, g_ref, qg_ref, kv_ref, pk_ref, sems):
    width = q_ref.shape[1]
    left, right = slice(0, width), slice(width, 2 * width)
    places = [(q_ref, qg_ref, left), (k_ref, kv_ref, left), (v_ref, kv_ref, right), (g_ref, qg_ref, right)]
    copies = [
        pltpu.make_async_copy(src, dst.at[:, cols], sems.at[i]) for i, (src, dst, cols) in enumerate(places)
    ]
    for copy in copies:
        copy.start()
    for copy in copies:
        copy.wait()
    row = lanes_of([biggest(dst[:, cols]) for _, dst, cols in places])
    pk_ref[...] = jnp.broadcast_to(row[None], pk_ref.shape)


def place_of(zh, groups, rows, s):
    return pl.ds(pl.multiple_of(lax.rem(zh + groups - s, groups) * rows, 16), rows)


def half_pass(heads, pk, qs, gs, kb, vb, e_ref):
    pq, pkk = pk[:, 0:1], pk[:, 1:2]
    score_scale = pq * pkk / (TOP * TOP * ROOT)
    to_power = score_scale * math.log2(math.e)
    found = []
    for h in range(heads):
        cols = slice(h * HD, (h + 1) * HD)
        s = mxu(kb[:, cols], qs[:, cols], NT)
        peak = jnp.max(s, axis=0, keepdims=True)
        e = jnp.exp2(s * to_power - peak * to_power)
        m = peak * score_scale
        weights = e.astype(BF16)
        e_ref[h] = weights
        total = jnp.sum(e, axis=0, keepdims=True)
        o = mxu(vb[:, cols], weights, TN) / total
        d = jnp.sum(o * gs[:, cols].T.astype(F32), axis=0, keepdims=True)
        found.append((m, m + jnp.log(total), d, o))
    return found


def load_keys(parts, pk, kb, vb):
    rows, width = parts[0].shape[0], kb.shape[1]
    for s, ref in enumerate(parts):
        kb[s * rows : (s + 1) * rows, :] = scaled(ref[:, :width], TOP / pk[:, 1:2])
        vb[s * rows : (s + 1) * rows, :] = scaled(ref[:, width:], TOP / pk[:, 2:3])


def near_kernel(heads, groups, zh_ref, *refs):
    near = (refs[0], refs[5], refs[2], refs[3])
    qgs = (refs[4], refs[1], refs[7], refs[6])
    pk_ref, qs, gs, kb, vb, e_ref, ot_ref, row_ref = refs[2 * groups :]
    rows, width = qgs[0].shape[0], qs.shape[1]
    pk = peak_lanes(pk_ref)
    zh = zh_ref[0]
    for s, ref in enumerate(qgs):
        qs[place_of(zh, groups, rows, s), :] = scaled(ref[:, :width], TOP / pk[:, 0:1])
        gs[place_of(zh, groups, rows, s), :] = scaled(ref[:, width:], TOP / pk[:, 3:4])
    load_keys(near, pk, kb, vb)
    row_ref[...] = jnp.zeros_like(row_ref)
    row_ref[PEAK_ROW : PEAK_ROW + 1, :128] = pk
    for h, (m, lse, d, o) in enumerate(half_pass(heads, pk, qs, gs, kb, vb, e_ref)):
        ot_ref[h * HD : (h + 1) * HD, :] = o
        for i, row in enumerate((m, lse, d)):
            row_ref[3 * h + i : 3 * h + i + 1, :] = row


def far_kernel(heads, groups, *refs):
    far = refs[:groups]
    qs, gs, ot1_ref, row1_ref, kb, vb, e_ref, ot_ref, row_ref, st_ref = refs[groups:]
    pk = row1_ref[PEAK_ROW : PEAK_ROW + 1, :128]
    load_keys(far, pk, kb, vb)
    row_ref[...] = jnp.zeros_like(row_ref)
    stats = []
    for h, (m, lse, d, o) in enumerate(half_pass(heads, pk, qs, gs, kb, vb, e_ref)):
        cols = slice(h * HD, (h + 1) * HD)
        lse1, d1 = (row1_ref[3 * h + i : 3 * h + i + 1, :] for i in (1, 2))
        top = jnp.maximum(lse, lse1)
        both = top + jnp.log(jnp.exp(lse - top) + jnp.exp(lse1 - top))
        w, w1 = jnp.exp(lse - both), jnp.exp(lse1 - both)
        ot_ref[cols, :] = w * o + w1 * ot1_ref[cols, :]
        row_ref[h : h + 1, :] = m
        stats += [both, w * d + w1 * d1]
    st_ref[...] = jnp.zeros_like(st_ref)
    for i, row in enumerate(stats):
        st_ref[i : i + 1, :] = row


def middle_kernel(heads, gs, vb1, vb2, dp1, dp2):
    for h in range(heads):
        cols = slice(h * HD, (h + 1) * HD)
        for vb, dp in ((vb1, dp1), (vb2, dp2)):
            dp[h] = mxu(vb[:, cols], gs[:, cols], NT)


def totals(sts, h):
    lses = [st[2 * h : 2 * h + 1, :] for st in sts]
    top = functools.reduce(jnp.maximum, lses)
    log_total = top + jnp.log(sum(jnp.exp(x - top) for x in lses))
    delta = sum(jnp.exp(x - log_total) * st[2 * h + 1 : 2 * h + 2, :] for x, st in zip(lses, sts))
    return log_total, delta


def keys_kernel(heads, groups, *refs):
    sts, dkvs = refs[:groups], refs[-groups:]
    qs, gs, e1, e2, row1_ref, row2_ref, dp1, dp2, ds1, ds2 = refs[groups:-groups]
    pk = row1_ref[PEAK_ROW : PEAK_ROW + 1, :128]
    pq, pkk, pv, pg = (pk[:, i : i + 1] for i in range(4))
    grad_scale = pg * pv / (TOP * TOP)
    width = qs.shape[1]
    rows = e1.shape[1] // groups
    for h in range(heads):
        left = slice(h * HD, (h + 1) * HD)
        right = slice(width + h * HD, width + (h + 1) * HD)
        log_total, delta = totals(sts, h)
        q, gt = qs[:, left], gs[:, left].astype(F32).T
        halves = ((e1, row1_ref[3 * h : 3 * h + 1, :], dp1, ds1), (e2, row2_ref[h : h + 1, :], dp2, ds2))
        for half, (e, m, dp, ds) in enumerate(halves):
            share = jnp.exp(m - log_total)
            slope = share * grad_scale
            dv = mxu(e[h], (gt * share).astype(BF16), NT) * (pg / TOP)
            d = (e[h].astype(F32) * (dp[h] * slope - delta * slope)).astype(BF16)
            ds[h] = d
            dk = mxu(d, q, NN) * (pq / (TOP * ROOT))
            for s, ref in enumerate(dkvs):
                part, to = slice(s * rows, (s + 1) * rows), slice(half * rows, (half + 1) * rows)
                ref[to, left] = dk[part].astype(BF16)
                ref[to, right] = dv[part].astype(BF16)


def queries_kernel(heads, groups, zh_ref, *refs):
    sts, (row1_ref, ot_ref, kb1, kb2, ds1, ds2) = refs[:groups], refs[groups : groups + 6]
    oqs, oqa = refs[groups + 6 : -1], refs[-1]
    rows, width = oqs[0].shape[0], kb1.shape[1]
    pk = row1_ref[PEAK_ROW : PEAK_ROW + 1, :128]
    for h in range(heads):
        left = slice(h * HD, (h + 1) * HD)
        right = slice(width + h * HD, width + (h + 1) * HD)
        log_total, _ = totals(sts, h)
        weight = jnp.exp(sts[0][2 * h : 2 * h + 1, :] - log_total) * (pk[:, 2:3] / TOP)
        oqa[:, left] = (ot_ref[left, :] * weight).astype(BF16).T
        dq = mxu(kb1[:, left], ds1[h], TN) + mxu(kb2[:, left], ds2[h], TN)
        dq = dq * (pk[:, 1:2] / (TOP * ROOT))
        oqa[:, right] = dq.astype(BF16).T
    for s, ref in enumerate(oqs):
        ref[...] = oqa[place_of(zh_ref[0], groups, rows, s), :]


def relay_kernel(a_ref, b_ref, sum_ref):
    sum_ref[...] = (a_ref[...].astype(F32) + b_ref[...].astype(F32)).astype(BF16)


def fold_kernel(*refs):
    parts, (own_ref, send_ref) = refs[:-2], refs[-2:]
    rows = own_ref.shape[0]
    own_ref[...] = sum(r[:rows, :].astype(F32) for r in parts)
    send_ref[...] = sum(r[rows:, :].astype(F32) for r in parts).astype(BF16)


def sums_kernel(own_ref, got_ref, *refs):
    *oqs, goq_ref, gkv_ref, pk_ref = refs
    width = own_ref.shape[1] // 2
    goq_ref[...] = sum(r[...].astype(F32) for r in oqs)
    gkv_ref[...] = own_ref[...] + got_ref[...].astype(F32)
    row = lanes_of([biggest(r[:, c]) for r in (goq_ref, gkv_ref) for c in (slice(0, width), slice(width, 2 * width))])
    pk_ref[...] = jnp.broadcast_to(row[None], pk_ref.shape)


def cast_kernel(goq_ref, gkv_ref, pk_ref, *outs):
    pk = peak_lanes(pk_ref)
    width = outs[0].shape[1]
    sources = [r[:, c] for r in (goq_ref, gkv_ref) for c in (slice(0, width), slice(width, 2 * width))]
    for i, (src, dst) in enumerate(zip(sources, outs)):
        dst[...] = scaled(src, TOP / pk[:, i : i + 1])


def shift(n, s):
    return [(i, (i + s) % n) for i in range(n)]


def spread(x, axis, n):
    return [x] + [lax.ppermute(x, axis, shift(n, s)) for s in range(1, n)]


def home(parts, axis):
    n = len(parts)
    return [parts[0]] + [lax.ppermute(parts[s], axis, shift(n, n - s)) for s in range(1, n)]


def like(dtype, *shape):
    return jax.ShapeDtypeStruct(shape, dtype)


def on_device(sizes, queries, keys, values, out_grad):
    groups, everyone = sizes["zh"], math.prod(sizes.values())
    axes = tuple(sizes)
    rows, width = queries.shape
    heads = width // HD
    q_rows, k_rows = rows * groups, rows * sizes["x"] * sizes["zl"]
    pairs = q_rows * k_rows * heads
    peaks = like(F32, everyone, 1, 128)
    wide = like(BF16, rows, 2 * width)
    zh = lax.axis_index("zh").astype(jnp.int32).reshape(1)
    smem = pl.BlockSpec(memory_space=pltpu.SMEM)
    vmem = pl.BlockSpec(memory_space=pltpu.VMEM)
    hbm = pl.BlockSpec(memory_space=pltpu.HBM)

    qg, kv, pk = call(
        prep_kernel,
        "prep",
        (wide, wide, peaks),
        (queries, keys, values, out_grad),
        [pltpu.SemaphoreType.DMA((4,))],
        nbytes=2**20,
        limit=PREP_LIMIT,
        in_specs=[hbm] * 4,
    )
    twin = lax.ppermute(kv, "zl", shift(2, 1))
    near = spread(kv, "x", sizes["x"])
    qgs = [qg, lax.ppermute(qg, "zh", shift(groups, 1)), None, lax.ppermute(qg, "zh", shift(groups, groups - 1))]
    qgs[2] = lax.ppermute(qgs[1], "zh", shift(groups, 1))
    far = spread(twin, "x", sizes["x"])
    pk = lax.all_to_all(pk, axes, 0, 0, tiled=True)
    half = like(BF16, q_rows, width)
    square = like(F32, heads, q_rows, q_rows)
    edges = like(BF16, heads, q_rows, q_rows)
    some_rows = like(F32, 16, q_rows)
    outputs = like(F32, width, q_rows)
    qs, gs, kb1, vb1, e1, ot1, row1 = call(
        functools.partial(near_kernel, heads, groups),
        "near",
        (half,) * 4 + (edges, outputs, some_rows),
        (zh, near[0], qgs[1], near[2], near[3], qgs[0], near[1], qgs[3], qgs[2], pk),
        flops=2 * pairs * HD,
        nbytes=4 * 2**20,
        exps=pairs // 2,
        limit=FORWARD_LIMIT,
        in_specs=[smem] + [vmem] * (2 * groups + 1),
    )
    kb2, vb2, e2, ot, row2, stats = call(
        functools.partial(far_kernel, heads, groups),
        "far",
        (half,) * 2 + (edges, outputs, some_rows, like(F32, 8, q_rows)),
        (*far, qs, gs, ot1, row1),
        flops=2 * pairs * HD,
        nbytes=4 * 2**20,
        exps=pairs // 2,
        limit=FORWARD_LIMIT,
    )
    sts = home([stats] * groups, "zh")
    dp1, dp2 = call(
        functools.partial(middle_kernel, heads),
        "middle",
        (square, square),
        (gs, vb1, vb2),
        flops=2 * pairs * HD,
        nbytes=8 * 2**20,
        limit=WORK_LIMIT,
    )
    ds1, ds2, *dkvs = call(
        functools.partial(keys_kernel, heads, groups),
        "keys",
        (edges, edges) + (like(BF16, 2 * rows, 2 * width),) * groups,
        (*sts, qs, gs, e1, e2, row1, row2, dp1, dp2),
        flops=4 * pairs * HD,
        nbytes=6 * 2**20,
        limit=WORK_LIMIT,
    )
    oqs = call(
        functools.partial(queries_kernel, heads, groups),
        "queries",
        (wide,) * groups,
        (zh, *sts, row1, ot, kb1, kb2, ds1, ds2),
        [pltpu.VMEM((q_rows, 2 * width), BF16)],
        flops=2 * pairs * HD,
        nbytes=6 * 2**20,
        limit=WORK_LIMIT,
        in_specs=[smem] + [vmem] * (groups + 6),
    )
    dkvs = home(dkvs, "x")
    ahead = lax.ppermute(oqs[2], "zh", shift(groups, groups - 1))
    back = lax.ppermute(oqs[3], "zh", shift(groups, 1))
    relay = call(relay_kernel, "relay", wide, (oqs[1], ahead), nbytes=2**20, limit=WORK_LIMIT)
    oqs = [oqs[0], back, lax.ppermute(relay, "zh", shift(groups, groups - 1))]
    own, send = call(fold_kernel, "fold", (like(F32, rows, 2 * width), wide), dkvs, nbytes=2 * 2**20)
    got = lax.ppermute(send, "zl", shift(2, 1))
    goq, gkv, tops = call(
        sums_kernel,
        "sums",
        (like(F32, rows, 2 * width), like(F32, rows, 2 * width), peaks),
        (own, got, *oqs),
        nbytes=3 * 2**20,
    )
    tops = lax.all_to_all(tops, axes, 0, 0, tiled=True)
    return call(cast_kernel, "cast", (like(BF16, rows, width),) * 4, (goq, gkv, tops), nbytes=2**20)


def solution(mesh):
    sizes = dict(x=4, zh=4, zl=2, y=4, c=2)
    fine = Mesh(mesh.devices.reshape(tuple(sizes.values())), tuple(sizes))
    spec = P(("x", "zh", "zl"), ("y", "c"))
    return jax.shard_map(
        functools.partial(on_device, sizes),
        mesh=fine,
        in_specs=(spec,) * 4,
        out_specs=(spec,) * 4,
        check_vma=False,
    )
```

```python
import functools
import math

import jax
import jax.numpy as jnp
from jax import lax
from jax.experimental import pallas as pl
from jax.experimental.pallas import tpu as pltpu
from jax.sharding import Mesh
from jax.sharding import PartitionSpec as P

HD = 128
TOP = 4.0
ROOT = math.sqrt(HD)
NT = (((1,), (1,)), ((), ()))
TN = (((0,), (0,)), ((), ()))
NN = (((1,), (0,)), ((), ()))
F32 = jnp.float32
BF16 = jnp.bfloat16
VMEM_LIMIT = 48 * 1024 * 1024
WORK_LIMIT = 24 * 1024 * 1024
PEAK_ROW = 15
FORWARD_LIMIT = 32 * 1024 * 1024
PREP_LIMIT = 62 * 1024 * 1024


def mxu(a, b, dims):
    return lax.dot_general(a, b, dims, preferred_element_type=F32)


def call(body, name, out_shape, args, scratch=(), flops=0, nbytes=0, exps=0, limit=VMEM_LIMIT, **more):
    return pl.pallas_call(
        body,
        name=name,
        out_shape=out_shape,
        scratch_shapes=list(scratch),
        **more,
        compiler_params=pltpu.CompilerParams(vmem_limit_bytes=limit),
        cost_estimate=pl.CostEstimate(flops=flops, bytes_accessed=nbytes, transcendentals=exps),
    )(*args)


def lanes_of(values):
    lane = lax.broadcasted_iota(jnp.int32, (1, 128), 1)
    row = jnp.zeros((1, 128), F32)
    for i, value in enumerate(values):
        row = jnp.where(lane == i, value, row)
    return row


def peak_lanes(ref):
    step = ref.shape[0] // 8
    parts = [jnp.max(ref[i * step : (i + 1) * step], axis=0) for i in range(8)]
    while len(parts) > 1:
        parts = [jnp.maximum(a, b) for a, b in zip(parts[::2], parts[1::2])]
    return parts[0]


def biggest(x):
    return jnp.max(jnp.abs(x.astype(F32)), keepdims=True)


def scaled(x, factor):
    return (x.astype(F32) * factor).astype(BF16)


def prep_kernel(q_ref, k_ref, v_ref, g_ref, qg_ref, kv_ref, pk_ref, sems):
    width = q_ref.shape[1]
    left, right = slice(0, width), slice(width, 2 * width)
    places = [(q_ref, qg_ref, left), (k_ref, kv_ref, left), (v_ref, kv_ref, right), (g_ref, qg_ref, right)]
    copies = [
        pltpu.make_async_copy(src, dst.at[:, cols], sems.at[i]) for i, (src, dst, cols) in enumerate(places)
    ]
    for copy in copies:
        copy.start()
    for copy in copies:
        copy.wait()
    row = lanes_of([biggest(dst[:, cols]) for _, dst, cols in places])
    pk_ref[...] = jnp.broadcast_to(row[None], pk_ref.shape)


def place_of(at_ref, groups, rows, s):
    where = lax.rem(at_ref[0] + 2 * groups - at_ref[1] * s, groups)
    return pl.ds(pl.multiple_of(where * rows, 16), rows)


def half_pass(heads, pk, qs, gs, kb, vb, e_ref):
    pq, pkk = pk[:, 0:1], pk[:, 1:2]
    score_scale = pq * pkk / (TOP * TOP * ROOT)
    to_power = score_scale * math.log2(math.e)
    found = []
    for h in range(heads):
        cols = slice(h * HD, (h + 1) * HD)
        s = mxu(kb[:, cols], qs[:, cols], NT)
        peak = jnp.max(s, axis=0, keepdims=True)
        e = jnp.exp2(s * to_power - peak * to_power)
        m = peak * score_scale
        weights = e.astype(BF16)
        e_ref[h] = weights
        total = jnp.sum(e, axis=0, keepdims=True)
        o = mxu(vb[:, cols], weights, TN) / total
        d = jnp.sum(o * gs[:, cols].T.astype(F32), axis=0, keepdims=True)
        found.append((m, m + jnp.log(total), d, o))
    return found


def load_keys(parts, pk, kb, vb):
    rows, width = parts[0].shape[0], kb.shape[1]
    for s, ref in enumerate(parts):
        kb[s * rows : (s + 1) * rows, :] = scaled(ref[:, :width], TOP / pk[:, 1:2])
        vb[s * rows : (s + 1) * rows, :] = scaled(ref[:, width:], TOP / pk[:, 2:3])


def near_kernel(heads, groups, at_ref, *refs):
    near = (refs[0], refs[5], refs[2], refs[3])
    qgs = (refs[4], refs[1], refs[7], refs[6])
    pk_ref, qs, gs, kb, vb, e_ref, ot_ref, row_ref = refs[2 * groups :]
    rows, width = qgs[0].shape[0], qs.shape[1]
    pk = peak_lanes(pk_ref)
    for s, ref in enumerate(qgs):
        qs[place_of(at_ref, groups, rows, s), :] = scaled(ref[:, :width], TOP / pk[:, 0:1])
        gs[place_of(at_ref, groups, rows, s), :] = scaled(ref[:, width:], TOP / pk[:, 3:4])
    load_keys(near, pk, kb, vb)
    row_ref[...] = jnp.zeros_like(row_ref)
    row_ref[PEAK_ROW : PEAK_ROW + 1, :128] = pk
    for h, (m, lse, d, o) in enumerate(half_pass(heads, pk, qs, gs, kb, vb, e_ref)):
        ot_ref[h * HD : (h + 1) * HD, :] = o
        for i, row in enumerate((m, lse, d)):
            row_ref[3 * h + i : 3 * h + i + 1, :] = row


def far_kernel(heads, groups, *refs):
    far = refs[:groups]
    qs, gs, ot1_ref, row1_ref, kb, vb, e_ref, ot_ref, row_ref, st_ref = refs[groups:]
    pk = row1_ref[PEAK_ROW : PEAK_ROW + 1, :128]
    load_keys(far, pk, kb, vb)
    row_ref[...] = jnp.zeros_like(row_ref)
    stats = []
    for h, (m, lse, d, o) in enumerate(half_pass(heads, pk, qs, gs, kb, vb, e_ref)):
        cols = slice(h * HD, (h + 1) * HD)
        lse1, d1 = (row1_ref[3 * h + i : 3 * h + i + 1, :] for i in (1, 2))
        top = jnp.maximum(lse, lse1)
        both = top + jnp.log(jnp.exp(lse - top) + jnp.exp(lse1 - top))
        w, w1 = jnp.exp(lse - both), jnp.exp(lse1 - both)
        ot_ref[cols, :] = w * o + w1 * ot1_ref[cols, :]
        row_ref[h : h + 1, :] = m
        stats += [both, w * d + w1 * d1]
    st_ref[...] = jnp.zeros_like(st_ref)
    for i, row in enumerate(stats):
        st_ref[i : i + 1, :] = row


def middle_kernel(heads, gs, vb1, vb2, dp1, dp2):
    for h in range(heads):
        cols = slice(h * HD, (h + 1) * HD)
        for vb, dp in ((vb1, dp1), (vb2, dp2)):
            dp[h] = mxu(vb[:, cols], gs[:, cols], NT)


def totals(sts, h):
    lses = [st[2 * h : 2 * h + 1, :] for st in sts]
    top = functools.reduce(jnp.maximum, lses)
    log_total = top + jnp.log(sum(jnp.exp(x - top) for x in lses))
    delta = sum(jnp.exp(x - log_total) * st[2 * h + 1 : 2 * h + 2, :] for x, st in zip(lses, sts))
    return log_total, delta


def keys_kernel(heads, groups, *refs):
    sts, dkvs = refs[:groups], refs[-groups:]
    qs, gs, e1, e2, row1_ref, row2_ref, dp1, dp2, ds1, ds2 = refs[groups:-groups]
    pk = row1_ref[PEAK_ROW : PEAK_ROW + 1, :128]
    pq, pkk, pv, pg = (pk[:, i : i + 1] for i in range(4))
    grad_scale = pg * pv / (TOP * TOP)
    width = qs.shape[1]
    rows = e1.shape[1] // groups
    for h in range(heads):
        left = slice(h * HD, (h + 1) * HD)
        right = slice(width + h * HD, width + (h + 1) * HD)
        log_total, delta = totals(sts, h)
        q, gt = qs[:, left], gs[:, left].astype(F32).T
        halves = ((e1, row1_ref[3 * h : 3 * h + 1, :], dp1, ds1), (e2, row2_ref[h : h + 1, :], dp2, ds2))
        for half, (e, m, dp, ds) in enumerate(halves):
            share = jnp.exp(m - log_total)
            slope = share * grad_scale
            dv = mxu(e[h], (gt * share).astype(BF16), NT) * (pg / TOP)
            d = (e[h].astype(F32) * (dp[h] * slope - delta * slope)).astype(BF16)
            ds[h] = d
            dk = mxu(d, q, NN) * (pq / (TOP * ROOT))
            for s, ref in enumerate(dkvs):
                part, to = slice(s * rows, (s + 1) * rows), slice(half * rows, (half + 1) * rows)
                ref[to, left] = dk[part].astype(BF16)
                ref[to, right] = dv[part].astype(BF16)


def queries_kernel(heads, groups, at_ref, *refs):
    sts, (row1_ref, ot_ref, kb1, kb2, ds1, ds2) = refs[:groups], refs[groups : groups + 6]
    oqs, oqa = refs[groups + 6 : -1], refs[-1]
    rows, width = oqs[0].shape[0], kb1.shape[1]
    pk = row1_ref[PEAK_ROW : PEAK_ROW + 1, :128]
    for h in range(heads):
        left = slice(h * HD, (h + 1) * HD)
        right = slice(width + h * HD, width + (h + 1) * HD)
        log_total, _ = totals(sts, h)
        weight = jnp.exp(sts[0][2 * h : 2 * h + 1, :] - log_total) * (pk[:, 2:3] / TOP)
        oqa[:, left] = (ot_ref[left, :] * weight).astype(BF16).T
        dq = mxu(kb1[:, left], ds1[h], TN) + mxu(kb2[:, left], ds2[h], TN)
        dq = dq * (pk[:, 1:2] / (TOP * ROOT))
        oqa[:, right] = dq.astype(BF16).T
    for s, ref in enumerate(oqs):
        ref[...] = oqa[place_of(at_ref, groups, rows, s), :]


def relay_kernel(a_ref, b_ref, sum_ref):
    sum_ref[...] = (a_ref[...].astype(F32) + b_ref[...].astype(F32)).astype(BF16)


def fold_kernel(*refs):
    parts, (own_ref, send_ref) = refs[:-2], refs[-2:]
    rows = own_ref.shape[0]
    own_ref[...] = sum(r[:rows, :].astype(F32) for r in parts)
    send_ref[...] = sum(r[rows:, :].astype(F32) for r in parts).astype(BF16)


def sums_kernel(own_ref, got_ref, *refs):
    *oqs, goq_ref, gkv_ref, pk_ref = refs
    width = own_ref.shape[1] // 2
    goq_ref[...] = sum(r[...].astype(F32) for r in oqs)
    gkv_ref[...] = own_ref[...] + got_ref[...].astype(F32)
    row = lanes_of([biggest(r[:, c]) for r in (goq_ref, gkv_ref) for c in (slice(0, width), slice(width, 2 * width))])
    pk_ref[...] = jnp.broadcast_to(row[None], pk_ref.shape)


def cast_kernel(goq_ref, gkv_ref, pk_ref, *outs):
    pk = peak_lanes(pk_ref)
    width = outs[0].shape[1]
    sources = [r[:, c] for r in (goq_ref, gkv_ref) for c in (slice(0, width), slice(width, 2 * width))]
    for i, (src, dst) in enumerate(zip(sources, outs)):
        dst[...] = scaled(src, TOP / pk[:, i : i + 1])


def shift(n, s):
    return [(i, (i + s) % n) for i in range(n)]


def spread(x, axis, n):
    return [x] + [lax.ppermute(x, axis, shift(n, s)) for s in range(1, n)]


def turn(x, n, s):
    pairs = [(2 * i + c, 2 * ((i + (s if c == 0 else -s)) % n) + c) for i in range(n) for c in range(2)]
    return lax.ppermute(x, ("zh", "c"), pairs)


def home(parts, axis):
    n = len(parts)
    return [parts[0]] + [lax.ppermute(parts[s], axis, shift(n, n - s)) for s in range(1, n)]


def like(dtype, *shape):
    return jax.ShapeDtypeStruct(shape, dtype)


def on_device(sizes, queries, keys, values, out_grad):
    groups, everyone = sizes["zh"], math.prod(sizes.values())
    axes = tuple(sizes)
    rows, width = queries.shape
    heads = width // HD
    q_rows, k_rows = rows * groups, rows * sizes["x"] * sizes["zl"]
    pairs = q_rows * k_rows * heads
    peaks = like(F32, everyone, 1, 128)
    wide = like(BF16, rows, 2 * width)
    step = 1 - 2 * lax.axis_index("c")
    at = jnp.stack([lax.axis_index("zh"), step]).astype(jnp.int32)
    smem = pl.BlockSpec(memory_space=pltpu.SMEM)
    vmem = pl.BlockSpec(memory_space=pltpu.VMEM)
    hbm = pl.BlockSpec(memory_space=pltpu.HBM)

    qg, kv, pk = call(
        prep_kernel,
        "prep",
        (wide, wide, peaks),
        (queries, keys, values, out_grad),
        [pltpu.SemaphoreType.DMA((4,))],
        nbytes=2**20,
        limit=PREP_LIMIT,
        in_specs=[hbm] * 4,
    )
    twin = lax.ppermute(kv, "zl", shift(2, 1))
    near = spread(kv, "x", sizes["x"])
    qgs = [qg, turn(qg, groups, 1), None, turn(qg, groups, -1)]
    qgs[2] = turn(qgs[1], groups, 1)
    far = spread(twin, "x", sizes["x"])
    pk = lax.all_to_all(pk, axes, 0, 0, tiled=True)
    half = like(BF16, q_rows, width)
    square = like(F32, heads, q_rows, q_rows)
    edges = like(BF16, heads, q_rows, q_rows)
    some_rows = like(F32, 16, q_rows)
    outputs = like(F32, width, q_rows)
    qs, gs, kb1, vb1, e1, ot1, row1 = call(
        functools.partial(near_kernel, heads, groups),
        "near",
        (half,) * 4 + (edges, outputs, some_rows),
        (at, near[0], qgs[1], near[2], near[3], qgs[0], near[1], qgs[3], qgs[2], pk),
        flops=2 * pairs * HD,
        nbytes=4 * 2**20,
        exps=pairs // 2,
        limit=FORWARD_LIMIT,
        in_specs=[smem] + [vmem] * (2 * groups + 1),
    )
    kb2, vb2, e2, ot, row2, stats = call(
        functools.partial(far_kernel, heads, groups),
        "far",
        (half,) * 2 + (edges, outputs, some_rows, like(F32, 8, q_rows)),
        (*far, qs, gs, ot1, row1),
        flops=2 * pairs * HD,
        nbytes=4 * 2**20,
        exps=pairs // 2,
        limit=FORWARD_LIMIT,
    )
    sts = home([stats] * groups, "zh")
    dp1, dp2 = call(
        functools.partial(middle_kernel, heads),
        "middle",
        (square, square),
        (gs, vb1, vb2),
        flops=2 * pairs * HD,
        nbytes=8 * 2**20,
        limit=WORK_LIMIT,
    )
    ds1, ds2, *dkvs = call(
        functools.partial(keys_kernel, heads, groups),
        "keys",
        (edges, edges) + (like(BF16, 2 * rows, 2 * width),) * groups,
        (*sts, qs, gs, e1, e2, row1, row2, dp1, dp2),
        flops=4 * pairs * HD,
        nbytes=6 * 2**20,
        limit=WORK_LIMIT,
    )
    oqs = call(
        functools.partial(queries_kernel, heads, groups),
        "queries",
        (wide,) * groups,
        (at, *sts, row1, ot, kb1, kb2, ds1, ds2),
        [pltpu.VMEM((q_rows, 2 * width), BF16)],
        flops=2 * pairs * HD,
        nbytes=6 * 2**20,
        limit=WORK_LIMIT,
        in_specs=[smem] + [vmem] * (groups + 6),
    )
    dkvs = home(dkvs, "x")
    ahead = turn(oqs[2], groups, -1)
    back = turn(oqs[3], groups, 1)
    relay = call(relay_kernel, "relay", wide, (oqs[1], ahead), nbytes=2**20, limit=WORK_LIMIT)
    oqs = [oqs[0], back, turn(relay, groups, -1)]
    own, send = call(fold_kernel, "fold", (like(F32, rows, 2 * width), wide), dkvs, nbytes=2 * 2**20)
    got = lax.ppermute(send, "zl", shift(2, 1))
    goq, gkv, tops = call(
        sums_kernel,
        "sums",
        (like(F32, rows, 2 * width), like(F32, rows, 2 * width), peaks),
        (own, got, *oqs),
        nbytes=3 * 2**20,
    )
    tops = lax.all_to_all(tops, axes, 0, 0, tiled=True)
    return call(cast_kernel, "cast", (like(BF16, rows, width),) * 4, (goq, gkv, tops), nbytes=2**20)


def solution(mesh):
    sizes = dict(x=4, zh=4, zl=2, y=4, c=2)
    fine = Mesh(mesh.devices.reshape(tuple(sizes.values())), tuple(sizes))
    spec = P(("x", "zh", "zl"), ("y", "c"))
    return jax.shard_map(
        functools.partial(on_device, sizes),
        mesh=fine,
        in_specs=(spec,) * 4,
        out_specs=(spec,) * 4,
        check_vma=False,
    )
```

```python
import functools
import math

import jax
import jax.numpy as jnp
from jax import lax
from jax.experimental import pallas as pl
from jax.experimental.pallas import tpu as pltpu
from jax.sharding import Mesh
from jax.sharding import PartitionSpec as P

HD = 128
TOP = 4.0
ROOT = math.sqrt(HD)
NT = (((1,), (1,)), ((), ()))
TN = (((0,), (0,)), ((), ()))
NN = (((1,), (0,)), ((), ()))
F32 = jnp.float32
BF16 = jnp.bfloat16
VMEM_LIMIT = 48 * 1024 * 1024
WORK_LIMIT = 24 * 1024 * 1024
PEAK_ROW = 15
FORWARD_LIMIT = 32 * 1024 * 1024
PREP_LIMIT = 62 * 1024 * 1024


def mxu(a, b, dims):
    return lax.dot_general(a, b, dims, preferred_element_type=F32)


def call(body, name, out_shape, args, scratch=(), flops=0, nbytes=0, exps=0, limit=VMEM_LIMIT, **more):
    return pl.pallas_call(
        body,
        name=name,
        out_shape=out_shape,
        scratch_shapes=list(scratch),
        **more,
        compiler_params=pltpu.CompilerParams(vmem_limit_bytes=limit),
        cost_estimate=pl.CostEstimate(flops=flops, bytes_accessed=nbytes, transcendentals=exps),
    )(*args)


def lanes_of(values):
    lane = lax.broadcasted_iota(jnp.int32, (1, 128), 1)
    row = jnp.zeros((1, 128), F32)
    for i, value in enumerate(values):
        row = jnp.where(lane == i, value, row)
    return row


def peak_lanes(ref):
    step = ref.shape[0] // 8
    parts = [jnp.max(ref[i * step : (i + 1) * step], axis=0) for i in range(8)]
    while len(parts) > 1:
        parts = [jnp.maximum(a, b) for a, b in zip(parts[::2], parts[1::2])]
    return parts[0]


def biggest(x):
    return jnp.max(jnp.abs(x.astype(F32)), keepdims=True)


def scaled(x, factor):
    return (x.astype(F32) * factor).astype(BF16)


def prep_kernel(q_ref, k_ref, v_ref, g_ref, qg_ref, kv_ref, pk_ref, sems):
    width = q_ref.shape[1]
    left, right = slice(0, width), slice(width, 2 * width)
    places = [(q_ref, qg_ref, left), (k_ref, kv_ref, left), (v_ref, kv_ref, right), (g_ref, qg_ref, right)]
    copies = [
        pltpu.make_async_copy(src, dst.at[:, cols], sems.at[i]) for i, (src, dst, cols) in enumerate(places)
    ]
    for copy in copies:
        copy.start()
    for copy in copies:
        copy.wait()
    row = lanes_of([biggest(dst[:, cols]) for _, dst, cols in places])
    pk_ref[...] = jnp.broadcast_to(row[None], pk_ref.shape)


def place_of(at_ref, groups, rows, s):
    where = lax.rem(at_ref[0] + 2 * groups - at_ref[1] * s, groups)
    return pl.ds(pl.multiple_of(where * rows, 16), rows)


def half_pass(heads, pk, qs, gs, kb, vb, e_ref):
    pq, pkk = pk[:, 0:1], pk[:, 1:2]
    score_scale = pq * pkk / (TOP * TOP * ROOT)
    to_power = score_scale * math.log2(math.e)
    found = []
    for h in range(heads):
        cols = slice(h * HD, (h + 1) * HD)
        s = mxu(kb[:, cols], qs[:, cols], NT)
        peak = jnp.max(s, axis=0, keepdims=True)
        e = jnp.exp2(s * to_power - peak * to_power)
        m = peak * score_scale
        weights = e.astype(BF16)
        e_ref[h] = weights
        total = jnp.sum(e, axis=0, keepdims=True)
        o = mxu(vb[:, cols], weights, TN) / total
        d = jnp.sum(o * gs[:, cols].T.astype(F32), axis=0, keepdims=True)
        found.append((m, m + jnp.log(total), d, o))
    return found


def load_keys(parts, pk, kb, vb):
    rows, width = parts[0].shape[0], kb.shape[1]
    for s, ref in enumerate(parts):
        kb[s * rows : (s + 1) * rows, :] = scaled(ref[:, :width], TOP / pk[:, 1:2])
        vb[s * rows : (s + 1) * rows, :] = scaled(ref[:, width:], TOP / pk[:, 2:3])


def near_kernel(heads, groups, at_ref, *refs):
    near = (refs[0], refs[5], refs[2], refs[3])
    qgs = (refs[4], refs[1], refs[7], refs[6])
    pk_ref, qs, gs, kb, vb, e_ref, ot_ref, row_ref = refs[2 * groups :]
    rows, width = qgs[0].shape[0], qs.shape[1]
    pk = peak_lanes(pk_ref)
    for s, ref in enumerate(qgs):
        qs[place_of(at_ref, groups, rows, s), :] = scaled(ref[:, :width], TOP / pk[:, 0:1])
        gs[place_of(at_ref, groups, rows, s), :] = scaled(ref[:, width:], TOP / pk[:, 3:4])
    load_keys(near, pk, kb, vb)
    row_ref[...] = jnp.zeros_like(row_ref)
    row_ref[PEAK_ROW : PEAK_ROW + 1, :128] = pk
    for h, (m, lse, d, o) in enumerate(half_pass(heads, pk, qs, gs, kb, vb, e_ref)):
        ot_ref[h * HD : (h + 1) * HD, :] = o
        for i, row in enumerate((m, lse, d)):
            row_ref[3 * h + i : 3 * h + i + 1, :] = row


def far_kernel(heads, groups, *refs):
    far = refs[:groups]
    qs, gs, ot1_ref, row1_ref, kb, vb, e_ref, ot_ref, row_ref, st_ref = refs[groups:]
    pk = row1_ref[PEAK_ROW : PEAK_ROW + 1, :128]
    load_keys(far, pk, kb, vb)
    row_ref[...] = jnp.zeros_like(row_ref)
    stats = []
    for h, (m, lse, d, o) in enumerate(half_pass(heads, pk, qs, gs, kb, vb, e_ref)):
        cols = slice(h * HD, (h + 1) * HD)
        lse1, d1 = (row1_ref[3 * h + i : 3 * h + i + 1, :] for i in (1, 2))
        top = jnp.maximum(lse, lse1)
        both = top + jnp.log(jnp.exp(lse - top) + jnp.exp(lse1 - top))
        w, w1 = jnp.exp(lse - both), jnp.exp(lse1 - both)
        ot_ref[cols, :] = w * o + w1 * ot1_ref[cols, :]
        row_ref[h : h + 1, :] = m
        stats += [both, w * d + w1 * d1]
    st_ref[...] = jnp.zeros_like(st_ref)
    for i, row in enumerate(stats):
        st_ref[i : i + 1, :] = row


def middle_kernel(heads, gs, vb1, vb2, dp1, dp2):
    for h in range(heads):
        cols = slice(h * HD, (h + 1) * HD)
        for vb, dp in ((vb1, dp1), (vb2, dp2)):
            dp[h] = mxu(vb[:, cols], gs[:, cols], NT)


def totals(sts, h):
    lses = [st[2 * h : 2 * h + 1, :] for st in sts]
    top = functools.reduce(jnp.maximum, lses)
    log_total = top + jnp.log(sum(jnp.exp(x - top) for x in lses))
    delta = sum(jnp.exp(x - log_total) * st[2 * h + 1 : 2 * h + 2, :] for x, st in zip(lses, sts))
    return log_total, delta


def keys_kernel(heads, groups, *refs):
    sts, dkvs = refs[:groups], refs[-groups:]
    qs, gs, e1, e2, row1_ref, row2_ref, dp1, dp2, ds1, ds2 = refs[groups:-groups]
    pk = row1_ref[PEAK_ROW : PEAK_ROW + 1, :128]
    pq, pkk, pv, pg = (pk[:, i : i + 1] for i in range(4))
    grad_scale = pg * pv / (TOP * TOP)
    width = qs.shape[1]
    rows = e1.shape[1] // groups
    for h in range(heads):
        left = slice(h * HD, (h + 1) * HD)
        right = slice(width + h * HD, width + (h + 1) * HD)
        log_total, delta = totals(sts, h)
        q, gt = qs[:, left], gs[:, left].astype(F32).T
        halves = ((e1, row1_ref[3 * h : 3 * h + 1, :], dp1, ds1), (e2, row2_ref[h : h + 1, :], dp2, ds2))
        for half, (e, m, dp, ds) in enumerate(halves):
            share = jnp.exp(m - log_total)
            slope = share * grad_scale
            dv = mxu(e[h], (gt * share).astype(BF16), NT) * (pg / TOP)
            d = (e[h].astype(F32) * (dp[h] * slope - delta * slope)).astype(BF16)
            ds[h] = d
            dk = mxu(d, q, NN) * (pq / (TOP * ROOT))
            for s, ref in enumerate(dkvs):
                part, to = slice(s * rows, (s + 1) * rows), slice(half * rows, (half + 1) * rows)
                ref[to, left] = dk[part].astype(BF16)
                ref[to, right] = dv[part].astype(BF16)


def queries_kernel(heads, groups, at_ref, *refs):
    sts, (row1_ref, ot_ref, kb1, kb2, ds1, ds2) = refs[:groups], refs[groups : groups + 6]
    oqs, oqa = refs[groups + 6 : -1], refs[-1]
    rows, width = oqs[0].shape[0], kb1.shape[1]
    pk = row1_ref[PEAK_ROW : PEAK_ROW + 1, :128]
    for h in range(heads):
        left = slice(h * HD, (h + 1) * HD)
        right = slice(width + h * HD, width + (h + 1) * HD)
        log_total, _ = totals(sts, h)
        weight = jnp.exp(sts[0][2 * h : 2 * h + 1, :] - log_total) * (pk[:, 2:3] / TOP)
        oqa[:, left] = (ot_ref[left, :] * weight).astype(BF16).T
        dq = mxu(kb1[:, left], ds1[h], TN) + mxu(kb2[:, left], ds2[h], TN)
        dq = dq * (pk[:, 1:2] / (TOP * ROOT))
        oqa[:, right] = dq.astype(BF16).T
    for s, ref in enumerate(oqs):
        ref[...] = oqa[place_of(at_ref, groups, rows, s), :]


def relay_kernel(a_ref, b_ref, sum_ref):
    sum_ref[...] = (a_ref[...].astype(F32) + b_ref[...].astype(F32)).astype(BF16)


def fold_kernel(*refs):
    parts, (own_ref, send_ref) = refs[:-2], refs[-2:]
    rows = own_ref.shape[0]
    own_ref[...] = sum(r[:rows, :].astype(F32) for r in parts)
    send_ref[...] = sum(r[rows:, :].astype(F32) for r in parts).astype(BF16)


def sums_kernel(own_ref, got_ref, *refs):
    *oqs, goq_ref, gkv_ref, pk_ref = refs
    width = own_ref.shape[1] // 2
    goq_ref[...] = sum(r[...].astype(F32) for r in oqs)
    gkv_ref[...] = own_ref[...] + got_ref[...].astype(F32)
    row = lanes_of([biggest(r[:, c]) for r in (goq_ref, gkv_ref) for c in (slice(0, width), slice(width, 2 * width))])
    pk_ref[...] = jnp.broadcast_to(row[None], pk_ref.shape)


def cast_kernel(goq_ref, gkv_ref, pk_ref, *outs):
    pk = peak_lanes(pk_ref)
    width = outs[0].shape[1]
    sources = [r[:, c] for r in (goq_ref, gkv_ref) for c in (slice(0, width), slice(width, 2 * width))]
    for i, (src, dst) in enumerate(zip(sources, outs)):
        dst[...] = scaled(src, TOP / pk[:, i : i + 1])


def shift(n, s):
    return [(i, (i + s) % n) for i in range(n)]


def spread(x, axis, n):
    return [x] + [lax.ppermute(x, axis, shift(n, s)) for s in range(1, n)]


def turn(x, n, s, axis="zh"):
    pairs = [(2 * i + c, 2 * ((i + (s if c == 0 else -s)) % n) + c) for i in range(n) for c in range(2)]
    return lax.ppermute(x, (axis, "c"), pairs)


def home(parts, axis):
    n = len(parts)
    return [parts[0]] + [lax.ppermute(parts[s], axis, shift(n, n - s)) for s in range(1, n)]


def like(dtype, *shape):
    return jax.ShapeDtypeStruct(shape, dtype)


def on_device(sizes, queries, keys, values, out_grad):
    groups, everyone = sizes["zh"], math.prod(sizes.values())
    axes = tuple(sizes)
    rows, width = queries.shape
    heads = width // HD
    q_rows, k_rows = rows * groups, rows * sizes["x"] * sizes["zl"]
    pairs = q_rows * k_rows * heads
    peaks = like(F32, everyone, 1, 128)
    wide = like(BF16, rows, 2 * width)
    step = 1 - 2 * lax.axis_index("c")
    at = jnp.stack([lax.axis_index("zh"), step]).astype(jnp.int32)
    smem = pl.BlockSpec(memory_space=pltpu.SMEM)
    vmem = pl.BlockSpec(memory_space=pltpu.VMEM)
    hbm = pl.BlockSpec(memory_space=pltpu.HBM)

    qg, kv, pk = call(
        prep_kernel,
        "prep",
        (wide, wide, peaks),
        (queries, keys, values, out_grad),
        [pltpu.SemaphoreType.DMA((4,))],
        nbytes=2**20,
        limit=PREP_LIMIT,
        in_specs=[hbm] * 4,
    )
    twin = lax.ppermute(kv, "zl", shift(2, 1))
    nx = sizes["x"]
    near = [kv, turn(kv, nx, 1, "x"), None, turn(kv, nx, -1, "x")]
    near[2] = turn(kv, nx, 2, "x")
    qgs = [qg, turn(qg, groups, 1), None, turn(qg, groups, -1)]
    qgs[2] = turn(qgs[1], groups, 1)
    far = [twin] + [turn(twin, nx, s, "x") for s in range(1, nx)]
    pk = lax.all_to_all(pk, axes, 0, 0, tiled=True)
    half = like(BF16, q_rows, width)
    square = like(F32, heads, q_rows, q_rows)
    edges = like(BF16, heads, q_rows, q_rows)
    some_rows = like(F32, 16, q_rows)
    outputs = like(F32, width, q_rows)
    qs, gs, kb1, vb1, e1, ot1, row1 = call(
        functools.partial(near_kernel, heads, groups),
        "near",
        (half,) * 4 + (edges, outputs, some_rows),
        (at, near[0], qgs[1], near[2], near[3], qgs[0], near[1], qgs[3], qgs[2], pk),
        flops=2 * pairs * HD,
        nbytes=4 * 2**20,
        exps=pairs // 2,
        limit=FORWARD_LIMIT,
        in_specs=[smem] + [vmem] * (2 * groups + 1),
    )
    kb2, vb2, e2, ot, row2, stats = call(
        functools.partial(far_kernel, heads, groups),
        "far",
        (half,) * 2 + (edges, outputs, some_rows, like(F32, 8, q_rows)),
        (*far, qs, gs, ot1, row1),
        flops=2 * pairs * HD,
        nbytes=4 * 2**20,
        exps=pairs // 2,
        limit=FORWARD_LIMIT,
    )
    sts = home([stats] * groups, "zh")
    dp1, dp2 = call(
        functools.partial(middle_kernel, heads),
        "middle",
        (square, square),
        (gs, vb1, vb2),
        flops=2 * pairs * HD,
        nbytes=8 * 2**20,
        limit=WORK_LIMIT,
    )
    ds1, ds2, *dkvs = call(
        functools.partial(keys_kernel, heads, groups),
        "keys",
        (edges, edges) + (like(BF16, 2 * rows, 2 * width),) * groups,
        (*sts, qs, gs, e1, e2, row1, row2, dp1, dp2),
        flops=4 * pairs * HD,
        nbytes=6 * 2**20,
        limit=WORK_LIMIT,
    )
    oqs = call(
        functools.partial(queries_kernel, heads, groups),
        "queries",
        (wide,) * groups,
        (at, *sts, row1, ot, kb1, kb2, ds1, ds2),
        [pltpu.VMEM((q_rows, 2 * width), BF16)],
        flops=2 * pairs * HD,
        nbytes=6 * 2**20,
        limit=WORK_LIMIT,
        in_specs=[smem] + [vmem] * (groups + 6),
    )
    dkvs = [dkvs[0]] + [turn(dkvs[s], nx, -s, "x") for s in range(1, nx)]
    ahead = turn(oqs[2], groups, -1)
    back = turn(oqs[3], groups, 1)
    relay = call(relay_kernel, "relay", wide, (oqs[1], ahead), nbytes=2**20, limit=WORK_LIMIT)
    oqs = [oqs[0], back, turn(relay, groups, -1)]
    own, send = call(fold_kernel, "fold", (like(F32, rows, 2 * width), wide), dkvs, nbytes=2 * 2**20)
    got = lax.ppermute(send, "zl", shift(2, 1))
    goq, gkv, tops = call(
        sums_kernel,
        "sums",
        (like(F32, rows, 2 * width), like(F32, rows, 2 * width), peaks),
        (own, got, *oqs),
        nbytes=3 * 2**20,
    )
    tops = lax.all_to_all(tops, axes, 0, 0, tiled=True)
    return call(cast_kernel, "cast", (like(BF16, rows, width),) * 4, (goq, gkv, tops), nbytes=2**20)


def solution(mesh):
    sizes = dict(x=4, zh=4, zl=2, y=4, c=2)
    fine = Mesh(mesh.devices.reshape(tuple(sizes.values())), tuple(sizes))
    spec = P(("x", "zh", "zl"), ("y", "c"))
    return jax.shard_map(
        functools.partial(on_device, sizes),
        mesh=fine,
        in_specs=(spec,) * 4,
        out_specs=(spec,) * 4,
        check_vma=False,
    )
```

```python
import functools
import math

import jax
import jax.numpy as jnp
from jax import lax
from jax.experimental import pallas as pl
from jax.experimental.pallas import tpu as pltpu
from jax.sharding import Mesh
from jax.sharding import PartitionSpec as P

HD = 128
TOP = 4.0
ROOT = math.sqrt(HD)
NT = (((1,), (1,)), ((), ()))
TN = (((0,), (0,)), ((), ()))
NN = (((1,), (0,)), ((), ()))
F32 = jnp.float32
BF16 = jnp.bfloat16
VMEM_LIMIT = 48 * 1024 * 1024
WORK_LIMIT = 24 * 1024 * 1024
PEAK_ROW = 15
FORWARD_LIMIT = 32 * 1024 * 1024
PREP_LIMIT = 62 * 1024 * 1024


def mxu(a, b, dims):
    return lax.dot_general(a, b, dims, preferred_element_type=F32)


def call(body, name, out_shape, args, scratch=(), flops=0, nbytes=0, exps=0, limit=VMEM_LIMIT, **more):
    return pl.pallas_call(
        body,
        name=name,
        out_shape=out_shape,
        scratch_shapes=list(scratch),
        **more,
        compiler_params=pltpu.CompilerParams(vmem_limit_bytes=limit),
        cost_estimate=pl.CostEstimate(flops=flops, bytes_accessed=nbytes, transcendentals=exps),
    )(*args)


def lanes_of(values):
    lane = lax.broadcasted_iota(jnp.int32, (1, 128), 1)
    row = jnp.zeros((1, 128), F32)
    for i, value in enumerate(values):
        row = jnp.where(lane == i, value, row)
    return row


def peak_lanes(ref):
    step = ref.shape[0] // 8
    parts = [jnp.max(ref[i * step : (i + 1) * step], axis=0) for i in range(8)]
    while len(parts) > 1:
        parts = [jnp.maximum(a, b) for a, b in zip(parts[::2], parts[1::2])]
    return parts[0]


def biggest(x):
    return jnp.max(jnp.abs(x.astype(F32)), keepdims=True)


def scaled(x, factor):
    return (x.astype(F32) * factor).astype(BF16)


def prep_kernel(q_ref, k_ref, v_ref, g_ref, qg_ref, kv_ref, pk_ref, sems):
    width = q_ref.shape[1]
    left, right = slice(0, width), slice(width, 2 * width)
    places = [(q_ref, qg_ref, left), (k_ref, kv_ref, left), (v_ref, kv_ref, right), (g_ref, qg_ref, right)]
    copies = [
        pltpu.make_async_copy(src, dst.at[:, cols], sems.at[i]) for i, (src, dst, cols) in enumerate(places)
    ]
    for copy in copies:
        copy.start()
    for copy in copies:
        copy.wait()
    row = lanes_of([biggest(dst[:, cols]) for _, dst, cols in places])
    pk_ref[...] = jnp.broadcast_to(row[None], pk_ref.shape)


def place_of(at_ref, groups, rows, s):
    where = lax.rem(at_ref[0] + 2 * groups - at_ref[1] * s, groups)
    return pl.ds(pl.multiple_of(where * rows, 16), rows)


def half_pass(heads, pk, qs, gs, kb, vb, e_ref):
    pq, pkk = pk[:, 0:1], pk[:, 1:2]
    score_scale = pq * pkk / (TOP * TOP * ROOT)
    to_power = score_scale * math.log2(math.e)
    found = []
    for h in range(heads):
        cols = slice(h * HD, (h + 1) * HD)
        s = mxu(kb[:, cols], qs[:, cols], NT)
        peak = jnp.max(s, axis=0, keepdims=True)
        e = jnp.exp2(s * to_power - peak * to_power)
        m = peak * score_scale
        weights = e.astype(BF16)
        e_ref[h] = weights
        total = jnp.sum(e, axis=0, keepdims=True)
        o = mxu(vb[:, cols], weights, TN) / total
        d = jnp.sum(o * gs[:, cols].T.astype(F32), axis=0, keepdims=True)
        found.append((m, m + jnp.log(total), d, o))
    return found


def load_keys(parts, pk, kb, vb):
    rows, width = parts[0].shape[0], kb.shape[1]
    for s, ref in enumerate(parts):
        kb[s * rows : (s + 1) * rows, :] = scaled(ref[:, :width], TOP / pk[:, 1:2])
        vb[s * rows : (s + 1) * rows, :] = scaled(ref[:, width:], TOP / pk[:, 2:3])


def near_kernel(heads, groups, at_ref, *refs):
    near = (refs[0], refs[5], refs[2], refs[3])
    qgs = (refs[4], refs[1], refs[7], refs[6])
    pk_ref, qs, gs, kb, vb, e_ref, ot_ref, row_ref = refs[2 * groups :]
    rows, width = qgs[0].shape[0], qs.shape[1]
    pk = peak_lanes(pk_ref)
    for s, ref in enumerate(qgs):
        qs[place_of(at_ref, groups, rows, s), :] = scaled(ref[:, :width], TOP / pk[:, 0:1])
        gs[place_of(at_ref, groups, rows, s), :] = scaled(ref[:, width:], TOP / pk[:, 3:4])
    load_keys(near, pk, kb, vb)
    row_ref[...] = jnp.zeros_like(row_ref)
    row_ref[PEAK_ROW : PEAK_ROW + 1, :128] = pk
    for h, (m, lse, d, o) in enumerate(half_pass(heads, pk, qs, gs, kb, vb, e_ref)):
        ot_ref[h * HD : (h + 1) * HD, :] = o
        for i, row in enumerate((m, lse, d)):
            row_ref[3 * h + i : 3 * h + i + 1, :] = row


def far_kernel(heads, groups, *refs):
    far = refs[:groups]
    qs, gs, ot1_ref, row1_ref, kb, vb, e_ref, ot_ref, row_ref, st_ref = refs[groups:]
    pk = row1_ref[PEAK_ROW : PEAK_ROW + 1, :128]
    load_keys(far, pk, kb, vb)
    row_ref[...] = jnp.zeros_like(row_ref)
    stats = []
    for h, (m, lse, d, o) in enumerate(half_pass(heads, pk, qs, gs, kb, vb, e_ref)):
        cols = slice(h * HD, (h + 1) * HD)
        lse1, d1 = (row1_ref[3 * h + i : 3 * h + i + 1, :] for i in (1, 2))
        top = jnp.maximum(lse, lse1)
        both = top + jnp.log(jnp.exp(lse - top) + jnp.exp(lse1 - top))
        w, w1 = jnp.exp(lse - both), jnp.exp(lse1 - both)
        ot_ref[cols, :] = w * o + w1 * ot1_ref[cols, :]
        row_ref[h : h + 1, :] = m
        stats += [both, w * d + w1 * d1]
    st_ref[...] = jnp.zeros_like(st_ref)
    for i, row in enumerate(stats):
        st_ref[i : i + 1, :] = row


def middle_kernel(heads, gs, vb1, vb2, dp1, dp2):
    for h in range(heads):
        cols = slice(h * HD, (h + 1) * HD)
        for vb, dp in ((vb1, dp1), (vb2, dp2)):
            dp[h] = mxu(vb[:, cols], gs[:, cols], NT)


def totals(sts, h):
    lses = [st[2 * h : 2 * h + 1, :] for st in sts]
    top = functools.reduce(jnp.maximum, lses)
    log_total = top + jnp.log(sum(jnp.exp(x - top) for x in lses))
    delta = sum(jnp.exp(x - log_total) * st[2 * h + 1 : 2 * h + 2, :] for x, st in zip(lses, sts))
    return log_total, delta


def keys_kernel(heads, groups, *refs):
    sts, dkvs = refs[:groups], refs[-groups:]
    qs, gs, e1, e2, row1_ref, row2_ref, dp1, dp2, ds1, ds2 = refs[groups:-groups]
    pk = row1_ref[PEAK_ROW : PEAK_ROW + 1, :128]
    pq, pkk, pv, pg = (pk[:, i : i + 1] for i in range(4))
    grad_scale = pg * pv / (TOP * TOP)
    width = qs.shape[1]
    rows = e1.shape[1] // groups
    for h in range(heads):
        left = slice(h * HD, (h + 1) * HD)
        right = slice(width + h * HD, width + (h + 1) * HD)
        log_total, delta = totals(sts, h)
        q, gt = qs[:, left], gs[:, left].astype(F32).T
        halves = ((e1, row1_ref[3 * h : 3 * h + 1, :], dp1, ds1), (e2, row2_ref[h : h + 1, :], dp2, ds2))
        for half, (e, m, dp, ds) in enumerate(halves):
            share = jnp.exp(m - log_total)
            slope = share * grad_scale
            dv = mxu(e[h], (gt * share).astype(BF16), NT) * (pg / TOP)
            d = (e[h].astype(F32) * (dp[h] * slope - delta * slope)).astype(BF16)
            ds[h] = d
            dk = mxu(d, q, NN) * (pq / (TOP * ROOT))
            for s, ref in enumerate(dkvs):
                part, to = slice(s * rows, (s + 1) * rows), slice(half * rows, (half + 1) * rows)
                ref[to, left] = dk[part].astype(BF16)
                ref[to, right] = dv[part].astype(BF16)


def queries_kernel(heads, groups, at_ref, *refs):
    sts, (row1_ref, ot_ref, kb1, kb2, ds1, ds2) = refs[:groups], refs[groups : groups + 6]
    oqs, oqa = refs[groups + 6 : -1], refs[-1]
    rows, width = oqs[0].shape[0], kb1.shape[1]
    pk = row1_ref[PEAK_ROW : PEAK_ROW + 1, :128]
    for h in range(heads):
        left = slice(h * HD, (h + 1) * HD)
        right = slice(width + h * HD, width + (h + 1) * HD)
        log_total, _ = totals(sts, h)
        weight = jnp.exp(sts[0][2 * h : 2 * h + 1, :] - log_total) * (pk[:, 2:3] / TOP)
        oqa[:, left] = (ot_ref[left, :] * weight).astype(BF16).T
        dq = mxu(kb1[:, left], ds1[h], TN) + mxu(kb2[:, left], ds2[h], TN)
        dq = dq * (pk[:, 1:2] / (TOP * ROOT))
        oqa[:, right] = dq.astype(BF16).T
    for s, ref in enumerate(oqs):
        ref[...] = oqa[place_of(at_ref, groups, rows, s), :]


def relay_kernel(a_ref, b_ref, sum_ref):
    sum_ref[...] = (a_ref[...].astype(F32) + b_ref[...].astype(F32)).astype(BF16)


def fold_kernel(*refs):
    parts, (own_ref, send_ref) = refs[:-2], refs[-2:]
    rows = own_ref.shape[0]
    own_ref[...] = sum(r[:rows, :].astype(F32) for r in parts)
    send_ref[...] = sum(r[rows:, :].astype(F32) for r in parts).astype(BF16)


def sums_kernel(own_ref, got_ref, *refs):
    *oqs, goq_ref, gkv_ref, pk_ref = refs
    width = own_ref.shape[1] // 2
    goq_ref[...] = sum(r[...].astype(F32) for r in oqs)
    gkv_ref[...] = own_ref[...] + got_ref[...].astype(F32)
    row = lanes_of([biggest(r[:, c]) for r in (goq_ref, gkv_ref) for c in (slice(0, width), slice(width, 2 * width))])
    pk_ref[...] = jnp.broadcast_to(row[None], pk_ref.shape)


def cast_kernel(goq_ref, gkv_ref, pk_ref, *outs):
    pk = peak_lanes(pk_ref)
    width = outs[0].shape[1]
    sources = [r[:, c] for r in (goq_ref, gkv_ref) for c in (slice(0, width), slice(width, 2 * width))]
    for i, (src, dst) in enumerate(zip(sources, outs)):
        dst[...] = scaled(src, TOP / pk[:, i : i + 1])


def shift(n, s):
    return [(i, (i + s) % n) for i in range(n)]


def spread(x, axis, n):
    return [x] + [lax.ppermute(x, axis, shift(n, s)) for s in range(1, n)]


def turn(x, n, s, axis="zh"):
    pairs = [(2 * i + c, 2 * ((i + (s if c == 0 else -s)) % n) + c) for i in range(n) for c in range(2)]
    return lax.ppermute(x, (axis, "c"), pairs)


def home(parts, axis):
    n = len(parts)
    return [parts[0]] + [lax.ppermute(parts[s], axis, shift(n, n - s)) for s in range(1, n)]


def like(dtype, *shape):
    return jax.ShapeDtypeStruct(shape, dtype)


def on_device(sizes, queries, keys, values, out_grad):
    groups, everyone = sizes["zh"], math.prod(sizes.values())
    axes = tuple(sizes)
    rows, width = queries.shape
    heads = width // HD
    q_rows, k_rows = rows * groups, rows * sizes["x"] * sizes["zl"]
    pairs = q_rows * k_rows * heads
    peaks = like(F32, everyone, 1, 128)
    wide = like(BF16, rows, 2 * width)
    step = 1 - 2 * lax.axis_index("c")
    at = jnp.stack([lax.axis_index("zh"), step]).astype(jnp.int32)
    smem = pl.BlockSpec(memory_space=pltpu.SMEM)
    vmem = pl.BlockSpec(memory_space=pltpu.VMEM)
    hbm = pl.BlockSpec(memory_space=pltpu.HBM)

    qg, kv, pk = call(
        prep_kernel,
        "prep",
        (wide, wide, peaks),
        (queries, keys, values, out_grad),
        [pltpu.SemaphoreType.DMA((4,))],
        nbytes=2**20,
        limit=PREP_LIMIT,
        in_specs=[hbm] * 4,
    )
    twin = lax.ppermute(kv, "zl", shift(2, 1))
    nx = sizes["x"]
    near = [kv, turn(kv, nx, 1, "x"), None, turn(kv, nx, -1, "x")]
    near[2] = turn(kv, nx, 2, "x")
    qgs = [qg, turn(qg, groups, 1), None, turn(qg, groups, -1)]
    qgs[2] = turn(qgs[1], groups, 1)
    far = [twin] + [turn(twin, nx, s, "x") for s in range(1, nx)]
    pk = lax.all_to_all(pk, axes, 0, 0, tiled=True)
    half = like(BF16, q_rows, width)
    square = like(F32, heads, q_rows, q_rows)
    edges = like(BF16, heads, q_rows, q_rows)
    some_rows = like(F32, 16, q_rows)
    outputs = like(F32, width, q_rows)
    qs, gs, kb1, vb1, e1, ot1, row1 = call(
        functools.partial(near_kernel, heads, groups),
        "near",
        (half,) * 4 + (edges, outputs, some_rows),
        (at, near[0], qgs[1], near[2], near[3], qgs[0], near[1], qgs[3], qgs[2], pk),
        flops=2 * pairs * HD,
        nbytes=4 * 2**20,
        exps=pairs // 2,
        limit=FORWARD_LIMIT,
        in_specs=[smem] + [vmem] * (2 * groups + 1),
    )
    kb2, vb2, e2, ot, row2, stats = call(
        functools.partial(far_kernel, heads, groups),
        "far",
        (half,) * 2 + (edges, outputs, some_rows, like(F32, 8, q_rows)),
        (*far, qs, gs, ot1, row1),
        flops=2 * pairs * HD,
        nbytes=4 * 2**20,
        exps=pairs // 2,
        limit=FORWARD_LIMIT,
    )
    sts = [stats] + [turn(stats, groups, -s) for s in range(1, groups)]
    dp1, dp2 = call(
        functools.partial(middle_kernel, heads),
        "middle",
        (square, square),
        (gs, vb1, vb2),
        flops=2 * pairs * HD,
        nbytes=8 * 2**20,
        limit=WORK_LIMIT,
    )
    ds1, ds2, *dkvs = call(
        functools.partial(keys_kernel, heads, groups),
        "keys",
        (edges, edges) + (like(BF16, 2 * rows, 2 * width),) * groups,
        (*sts, qs, gs, e1, e2, row1, row2, dp1, dp2),
        flops=4 * pairs * HD,
        nbytes=6 * 2**20,
        limit=WORK_LIMIT,
    )
    oqs = call(
        functools.partial(queries_kernel, heads, groups),
        "queries",
        (wide,) * groups,
        (at, *sts, row1, ot, kb1, kb2, ds1, ds2),
        [pltpu.VMEM((q_rows, 2 * width), BF16)],
        flops=2 * pairs * HD,
        nbytes=6 * 2**20,
        limit=WORK_LIMIT,
        in_specs=[smem] + [vmem] * (groups + 6),
    )
    dkvs = [dkvs[0]] + [turn(dkvs[s], nx, -s, "x") for s in range(1, nx)]
    ahead = turn(oqs[2], groups, -1)
    back = turn(oqs[3], groups, 1)
    relay = call(relay_kernel, "relay", wide, (oqs[1], ahead), nbytes=2**20, limit=WORK_LIMIT)
    oqs = [oqs[0], back, turn(relay, groups, -1)]
    own, send = call(fold_kernel, "fold", (like(F32, rows, 2 * width), wide), dkvs, nbytes=2 * 2**20)
    got = lax.ppermute(send, "zl", shift(2, 1))
    goq, gkv, tops = call(
        sums_kernel,
        "sums",
        (like(F32, rows, 2 * width), like(F32, rows, 2 * width), peaks),
        (own, got, *oqs),
        nbytes=3 * 2**20,
    )
    tops = lax.all_to_all(tops, axes, 0, 0, tiled=True)
    return call(cast_kernel, "cast", (like(BF16, rows, width),) * 4, (goq, gkv, tops), nbytes=2**20)


def solution(mesh):
    sizes = dict(x=4, zh=4, zl=2, y=4, c=2)
    fine = Mesh(mesh.devices.reshape(tuple(sizes.values())), tuple(sizes))
    spec = P(("x", "zh", "zl"), ("y", "c"))
    return jax.shard_map(
        functools.partial(on_device, sizes),
        mesh=fine,
        in_specs=(spec,) * 4,
        out_specs=(spec,) * 4,
        check_vma=False,
    )
```
